32 devices in a mesh: ctx: 8 (over z, y), tp: 4 (over x, core).
Axes of the slice: x: 2, y: 2, z: 4, core: 2. Of those that a mesh axis runs over, the one named last changes fastest.
Arguments:
- queries: bfloat16 [1024, 8192], P('ctx', 'tp'), may hold values from -56 to 56
- suffix_kv: bfloat16 [2, 1024, 1024], P(None, 'ctx', 'tp'), may hold values from -6 to 6
- cache_pool: bfloat16 [2, 128, 128, 1024], P(None, 'ctx', None, 'tp'), may hold values from -6 to 6
- hit_count: int32 [8], replicated, may hold values from 1 to 3, as said below
- hit_slots: int32 [8, 3], P('ctx'), may hold values from 0 to 15, as said below
- out_weight: bfloat16 [8192, 8192], P('tp', 'ctx'), may hold values from -1.1953125 to 1.1953125
Outputs:
- layer_out: bfloat16 [1024, 8192], P('tp', 'ctx')
The draws below stay inside these ranges and needn't reach their ends.
Inputs may be any that keep to these rules, and one draw needn't show every extreme that they name: hit_count[h] blocks of holder h belong to the prefix; some holder has exactly 3. `hit_slots`: row h names 3 distinct slots of holder h's pool; only its first hit_count[h] entries are hits, the others are unused.
All inputs are finite; a program needn't handle non-finite values.
Results may differ from the reference program's by a relative error of at most 0.024.
Values may be sent and summed in bfloat16 or wider, within the bound.
No kernel may reach another device: no remote copies, remote signals or barrier semaphores. Data moves between devices by JAX's collectives and lax.ppermute only.
A program may use at most 64 MiB of HBM per device.

```python
import math
import jax
import jax.numpy as jnp
from jax import lax

D = 8192
HQ = 64
HD = 128
BLK = 128
HCAP = 3
HOLD = 16
SLOTS = 8
SPAN = 1024
N_CTX = 8


def draw_queries(key, part):
    key = jax.random.fold_in(key, 1)
    values = jnp.clip(2.0 * jax.random.normal(key, (SPAN, HQ * HD), jnp.float32), -8.0, 8.0)
    return values.astype(jnp.bfloat16)


def draw_suffix_kv(key, part):
    key = jax.random.fold_in(key, 2)
    values = jnp.clip(jax.random.normal(key, (2, SPAN, SLOTS * HD), jnp.float32), -4.0, 4.0)
    return values.astype(jnp.bfloat16)


def draw_hit_count(key, part):
    key = jax.random.fold_in(key, 3)
    count_key, forced_key = jax.random.split(key)
    counts = jax.random.randint(count_key, (N_CTX,), 1, HCAP + 1, jnp.int32)
    forced = jax.random.randint(forced_key, (), 0, N_CTX, jnp.int32)
    return jnp.where(jnp.arange(N_CTX, dtype=jnp.int32) == forced, HCAP, counts).astype(jnp.int32)


def draw_hit_slots(key, part):
    key = jax.random.fold_in(key, 4)
    scores = jax.random.randint(key, (N_CTX, HOLD), 0, 1 << 20, jnp.int32) * HOLD + jnp.arange(HOLD, dtype=jnp.int32)[None, :]
    ranking = jnp.argsort(scores, axis=1, stable=True)
    return ranking[:, :HCAP].astype(jnp.int32)


def levels(key, dims, cuts, smallest, high):
    loudness = 1.0
    for position, blocks in cuts:
        steps = jax.random.uniform(jax.random.fold_in(jax.random.fold_in(key, 6), position), (blocks,), jnp.float32, smallest / len(cuts), high / len(cuts))
        loudness = loudness * jnp.repeat(jnp.exp(steps), dims[position] // blocks).reshape((-1,) + (1,) * (len(dims) - 1 - position))
    return loudness


def bell_draw(rng, shape, width, reach, cuts=(), held_as=jnp.bfloat16):
    factor_of = levels(rng, shape, cuts, -0.22, 0.18) if cuts else 1.0
    drawn = jax.random.normal(rng, shape, jnp.float32) * width * factor_of
    return jnp.minimum(jnp.maximum(drawn, -reach), reach).astype(held_as)


def setup_inputs(seed: int = 0) -> dict:
    arg_keys = jax.random.split(jax.random.key(seed), 7)
    queries = draw_queries(jax.random.fold_in(arg_keys[6], 71), 0)
    suffix_kv = draw_suffix_kv(jax.random.fold_in(arg_keys[6], 71), 0)
    cache_pool = bell_draw(arg_keys[2], (2, N_CTX * HOLD, BLK, SLOTS * HD), 1.0, 6.0, ((1, 8), (3, 4)))
    hit_count = draw_hit_count(jax.random.fold_in(arg_keys[6], 71), 0)
    hit_slots = draw_hit_slots(jax.random.fold_in(arg_keys[6], 71), 0)
    out_weight = bell_draw(arg_keys[5], (HQ * HD, D), 0.2, 1.1953125, ((0, 4), (1, 8)))
    return dict(queries=queries, suffix_kv=suffix_kv, cache_pool=cache_pool, hit_count=hit_count, hit_slots=hit_slots, out_weight=out_weight)


def reference(queries, suffix_kv, cache_pool, hit_count, hit_slots, out_weight):
    holders = jnp.arange(N_CTX, dtype=jnp.int32)
    pool_index = (holders[:, None] * HOLD + hit_slots).reshape(-1).astype(jnp.int32)
    picked = jnp.take(cache_pool, pool_index, axis=1)
    prefix = picked.reshape(2, N_CTX * HCAP * BLK, SLOTS * HD)
    kept_slots = jnp.arange(HCAP, dtype=jnp.int32)[None, :] < hit_count[:, None]
    prefix_ok = jnp.repeat(kept_slots.reshape(-1), BLK)
    every_key = jnp.concatenate([prefix, suffix_kv], axis=1)
    token_pos = jnp.arange(SPAN, dtype=jnp.int32)
    visible = jnp.concatenate([jnp.broadcast_to(prefix_ok[None, :], (SPAN, prefix.shape[1])), token_pos[None, :] <= token_pos[:, None]], axis=1)
    group_size = HQ // SLOTS

    def one_head(head_index):
        slot_index = head_index // group_size
        query_rows = lax.dynamic_slice_in_dim(queries, head_index * HD, HD, 1)
        key_rows = lax.dynamic_slice_in_dim(every_key[0], slot_index * HD, HD, 1)
        value_rows = lax.dynamic_slice_in_dim(every_key[1], slot_index * HD, HD, 1)
        scores = jnp.dot(query_rows, key_rows.T, preferred_element_type=jnp.float32) / math.sqrt(HD)
        scores = jnp.where(visible, scores, -1e+30)
        row_max = lax.optimization_barrier(jnp.max(scores, axis=1, keepdims=True))
        weights = jnp.where(visible, jnp.exp(scores - row_max), 0.0)
        row_total = lax.optimization_barrier(jnp.sum(weights, axis=1, keepdims=True))
        mixed_rows = jnp.dot(weights.astype(jnp.bfloat16), value_rows, preferred_element_type=jnp.float32)
        return (mixed_rows / row_total).astype(jnp.bfloat16)
    per_head = lax.map(one_head, jnp.arange(HQ, dtype=jnp.int32))
    attention = per_head.transpose(1, 0, 2).reshape(SPAN, HQ * HD)
    return jnp.dot(attention, out_weight, preferred_element_type=jnp.float32).astype(jnp.bfloat16)
```

```python
import functools
import math

import jax
import jax.numpy as jnp
from jax import lax
from jax.experimental import pallas as pl
from jax.experimental.pallas import tpu as pltpu
from jax.sharding import PartitionSpec as P

HD = 128
HCAP = 3
neg_fill = -1e30
score_scale = 1.0 / math.sqrt(HD)
kernel_vmem = 16 * 1024 * 1024

vmem = pl.BlockSpec(memory_space=pltpu.VMEM)
smem = pl.BlockSpec(memory_space=pltpu.SMEM)
hbm = pl.BlockSpec(memory_space=pltpu.HBM)
params = pltpu.CompilerParams(vmem_limit_bytes=kernel_vmem)
light = pl.CostEstimate(flops=1000, bytes_accessed=1000, transcendentals=0)


def ring_order(n):
    return [2 * q if 2 * q < n else 2 * (n - 1 - q) + 1 for q in range(n)]


def owner_of(me, step, n):
    place = jnp.where(me % 2 == 0, me // 2, n - 1 - me // 2)
    place = lax.rem(place + step + n, n)
    return jnp.where(2 * place < n, 2 * place, 2 * (n - 1 - place) + 1)


def pick_kernel(blk, hit_slots, pool_ref, suffix_ref, near_ref, rest_ref, held, slots_ref, slots_sem, sems):
    outs = (near_ref, rest_ref)
    fetch = pltpu.make_async_copy(hit_slots, slots_ref, slots_sem)
    fetch.start()
    fetch.wait()
    copies = []
    for kv in range(2):
        for place in range(HCAP + 1):
            if place == 0:
                src = suffix_ref.at[kv]
            else:
                src = pool_ref.at[kv, slots_ref[0, place - 1]]
            if kv == 0:
                dst = outs[place // 2].at[0, pl.ds(place % 2 * blk, blk), :]
            else:
                dst = held.at[place]
            copies.append(pltpu.make_async_copy(src, dst, sems.at[kv, place]))
    for copy in copies:
        copy.start()
    for copy in copies:
        copy.wait()
    for place in range(HCAP + 1):
        for lane in range(0, held.shape[2], HD):
            at = slice(place % 2 * blk, (place % 2 + 1) * blk)
            outs[place // 2][1, at, lane : lane + HD] = held[place, :, lane : lane + HD].T


def pick(hit_slots, cache_pool, suffix_kv):
    blk, wide = cache_pool.shape[2:]
    return pl.pallas_call(
        functools.partial(pick_kernel, blk),
        out_shape=[jax.ShapeDtypeStruct((2, 2 * blk, wide), jnp.bfloat16)] * 2,
        in_specs=[hbm, hbm, hbm],
        out_specs=[vmem, vmem],
        scratch_shapes=[
            pltpu.VMEM((HCAP + 1, blk, wide), jnp.bfloat16),
            pltpu.SMEM(hit_slots.shape, jnp.int32),
            pltpu.SemaphoreType.DMA,
            pltpu.SemaphoreType.DMA((2, HCAP + 1)),
        ],
        compiler_params=pltpu.CompilerParams(vmem_limit_bytes=60 * 1024 * 1024),
        name="pick",
    )(hit_slots, cache_pool, suffix_kv)


def fold(op, array):
    parts = [array[r : r + 8] for r in range(0, array.shape[0], 8)]
    while len(parts) > 1:
        pairs = [op(a, b) for a, b in zip(parts[::2], parts[1::2])]
        parts = pairs + parts[len(parts) - len(parts) % 2 :]
    return parts[0]


def flash_kernel(n, tok, pieces, first, last, hit_ref, q_ref, *refs):
    count = len(pieces)
    kv_refs, refs = refs[:count], refs[count:]
    me = lax.axis_index("ctx")
    heads = (q_ref.shape[1] if first else q_ref.shape[1] // tok * HD) // HD
    keys, wide = kv_refs[0].shape[1:]
    blk = keys // 2
    slots_dev = wide // HD
    group = heads // slots_dev
    per = 2 if group % 2 == 0 else 1
    rows = per * tok
    biases = []
    for kind, step in pieces:
        owner = owner_of(me, step, n)
        if kind == 0:
            seen = [None if step == 0 else owner < me, None]
        else:
            seen = [hit_ref[owner] > 1, hit_ref[owner] > 2]
        biases.append([0.0 if s is None else jnp.where(s, 0.0, neg_fill) for s in seen])

    def place(j):
        head = j * per
        cols = [slice((head + h) * HD, (head + h + 1) * HD) for h in range(per)]
        slot = head // group
        return cols, slice(head * tok, head * tok + rows), slice(slot * HD, (slot + 1) * HD)

    def score(j):
        cols, at, lanes = place(j)
        if first:
            turned = jnp.concatenate([q_ref[:, c].T for c in cols], axis=1)
            refs[-4][:, at] = turned
        else:
            turned = q_ref[:, at]
        scores = []
        for (kind, step), ref, bias in zip(pieces, kv_refs, biases):
            raw = jnp.dot(ref[0, :, lanes], turned, preferred_element_type=jnp.float32)
            for b in range(2):
                part = raw[b * blk : (b + 1) * blk]
                if (kind, step, b) == (0, 0, 0):
                    key = lax.broadcasted_iota(jnp.int32, part.shape, 0)
                    token = lax.broadcasted_iota(jnp.int32, part.shape, 1) % tok
                    part = jnp.where(key <= token, part, neg_fill)
                scores.append((part, bias[b]))
        return scores

    def weigh(j, scores):
        _, at, _ = place(j)
        tops = [fold(jnp.maximum, part) + bias for part, bias in scores]
        top = jnp.max(functools.reduce(jnp.maximum, tops), axis=0, keepdims=True)
        total = fade = None
        if not first:
            m_in, l_in, _ = refs[:3]
            old_top = m_in[:, at]
            top = jnp.maximum(old_top, top)
            fade = jnp.exp((old_top - top) * score_scale)
            total = l_in[:, at] * fade
        if not last:
            refs[-3][:, at] = jnp.broadcast_to(top, (8, rows))
        offset = top[:1] * score_scale
        probs = []
        for part, bias in scores:
            weights = jnp.exp(part * score_scale - (offset - bias))
            add = fold(jnp.add, weights)
            total = add if total is None else total + add
            probs.append(weights.astype(jnp.bfloat16))
        if not last:
            refs[-2][:, at] = total
        return jnp.concatenate(probs, axis=0), fade, total

    def mix(j, probs, fade, total):
        cols, at, lanes = place(j)
        values = [ref[1, b * blk : (b + 1) * blk, lanes] for ref in kv_refs for b in range(2)]
        mixed = jnp.dot(
            jnp.concatenate(values, axis=1), probs, preferred_element_type=jnp.float32
        )
        if not first:
            mixed = mixed + refs[2][:, at] * fade[:1]
        if not last:
            refs[-1][:, at] = mixed
            return
        result = mixed * (1.0 / jnp.sum(total, axis=0, keepdims=True))
        half = tok // 2
        for h, c in enumerate(cols):
            head_out = result[:, h * tok : (h + 1) * tok].T.astype(jnp.bfloat16)
            for k, out in enumerate(refs[-2:]):
                out[:, c] = head_out[k * half : (k + 1) * half]

    blocks = heads // per
    ahead = min(2, blocks)
    scores = [score(j) for j in range(ahead)]
    for j in range(blocks):
        weighed = weigh(j, scores[j])
        scores[j] = None
        if j + ahead < blocks:
            scores.append(score(j + ahead))
        mix(j, *weighed)


def flash(n, tok, queries, hit_count, pieces, arrays, state, last):
    rows = queries.size // HD
    small = jax.ShapeDtypeStruct((8, rows), jnp.float32)
    if last:
        out_shape = [jax.ShapeDtypeStruct((tok // 2, rows // tok * HD), jnp.bfloat16)] * 2
        aliases = {}
    else:
        out_shape = [small, small, jax.ShapeDtypeStruct((HD, rows), jnp.float32)]
        aliases = {2 + len(arrays) + i: i for i in range(len(state))}
    if not state:
        out_shape = [jax.ShapeDtypeStruct((HD, rows), jnp.bfloat16)] + out_shape
    return pl.pallas_call(
        functools.partial(flash_kernel, n, tok, pieces, not state, last),
        out_shape=out_shape,
        in_specs=[smem] + [vmem] * (1 + len(arrays) + len(state)),
        out_specs=[vmem] * len(out_shape),
        input_output_aliases=aliases,
        compiler_params=params,
        cost_estimate=light,
        name="flash",
    )(hit_count, queries, *arrays, *state)


def project_kernel(count, *refs):
    shard_refs, (w_ref, keep_ref, send_ref) = refs[: 2 * count], refs[2 * count :]
    odd = lax.axis_index("tp") % 2
    rows = jnp.concatenate([ref[...] for ref in shard_refs], axis=0)
    half = rows.shape[0] // (2 * count)
    wide = w_ref.shape[1]
    width = min(256, wide)
    for col in range(0, wide, width):
        at = slice(col, col + width)
        product = jnp.dot(rows, w_ref[:, at], preferred_element_type=jnp.float32)
        product = product.astype(jnp.bfloat16)
        for i in range(count):
            low = product[2 * i * half : (2 * i + 1) * half]
            high = product[(2 * i + 1) * half : (2 * i + 2) * half]

            @pl.when(odd == 0)
            def _():
                keep_ref[i, :, at] = low
                send_ref[i, :, at] = high

            @pl.when(odd == 1)
            def _():
                keep_ref[i, :, at] = high
                send_ref[i, :, at] = low


def project(arrays, out_weight):
    half = arrays[0].shape[0]
    depth, wide = out_weight.shape
    count = len(arrays) // 2
    return pl.pallas_call(
        functools.partial(project_kernel, count),
        out_shape=[jax.ShapeDtypeStruct((count, half, wide), jnp.bfloat16)] * 2,
        in_specs=[vmem] * (len(arrays) + 1),
        out_specs=[vmem, vmem],
        compiler_params=params,
        cost_estimate=light,
        name="project",
    )(*arrays, out_weight)


def sides(n, n_tp, steps):
    me = lax.axis_index("ctx")
    my_tp = lax.axis_index("tp")
    share = n // n_tp
    found, near_count, away_count = [], jnp.int32(0), jnp.int32(0)
    for step in steps:
        owner = owner_of(me, step, n)
        away = lax.bitwise_xor(owner // share, my_tp) // 2 % 2
        found.append((owner, away, jnp.where(away == 1, away_count, near_count)))
        near_count = near_count + 1 - away
        away_count = away_count + away
    return found


def added(a, b):
    return a.astype(jnp.float32) + b.astype(jnp.float32)


def sort_kernel(n, n_tp, steps, *refs):
    *refs, stay_ref, send_ref, last_stay_ref, last_send_ref = refs
    count = len(refs) // 2
    places = [(a, b, i) for a, b in zip(refs[:count], refs[count:]) for i in range(a.shape[0])]
    full = stay_ref.shape[0]
    for (a, b, i), (_, away, rank) in zip(places, sides(n, n_tp, steps)):
        total = added(a[i], b[i]).astype(jnp.bfloat16)
        for side, out, last in ((0, stay_ref, last_stay_ref), (1, send_ref, last_send_ref)):

            @pl.when((away == side) & (rank < full))
            def _():
                out[rank] = total

            @pl.when((away == side) & (rank == full))
            def _():
                last[0] = total


def sort(n, n_tp, steps, sums):
    keeps, gots = zip(*sums)
    half, wide = keeps[0].shape[1:]
    many = jax.ShapeDtypeStruct((n // 2 - 1, half, wide), jnp.bfloat16)
    one = jax.ShapeDtypeStruct((1, half, wide), jnp.bfloat16)
    return pl.pallas_call(
        functools.partial(sort_kernel, n, n_tp, steps),
        out_shape=[many, many, one, one],
        in_specs=[vmem] * (2 * len(sums)),
        out_specs=[vmem] * 4,
        compiler_params=params,
        cost_estimate=light,
        name="sort",
    )(*keeps, *gots)


def last_kernel(n, n_tp, keep_ref, got_ref, stay_in, send_in, stay_ref, send_ref):
    ((_, away, _),) = sides(n, n_tp, (n // 2,))
    total = added(keep_ref[...], got_ref[...]).astype(jnp.bfloat16)
    stay_ref[...] = jnp.where(away == 0, total, stay_in[...])
    send_ref[...] = jnp.where(away == 1, total, send_in[...])


def place_last(n, n_tp, keep, got, stay, send):
    return pl.pallas_call(
        functools.partial(last_kernel, n, n_tp),
        out_shape=[jax.ShapeDtypeStruct(keep.shape, jnp.bfloat16)] * 2,
        in_specs=[vmem] * 4,
        out_specs=[vmem] * 2,
        compiler_params=params,
        cost_estimate=light,
        name="last",
    )(keep, got, stay, send)


def choose_kernel(n, n_tp, steps, *refs):
    stay, got, last_stay, last_got, mine_ref, give_ref = refs
    my_tp = lax.axis_index("tp")
    share = n // n_tp
    found = sides(n, n_tp, steps)
    full = stay.shape[0]
    for r in range(full + 1):
        owner = jnp.int32(0)
        for candidate, away, rank in found:
            owner = jnp.where((away == 0) & (rank == r), candidate, owner)
        if r < full:
            total = added(stay[r], got[r])
        else:
            total = added(last_stay[0], last_got[0])
        for out, block in ((mine_ref, my_tp), (give_ref, lax.bitwise_xor(my_tp, 1))):

            @pl.when(owner // share == block)
            def _():
                out[owner % share] = total.astype(out.dtype)


def choose(n, n_tp, steps, arrays):
    half, wide = arrays[0].shape[1:]
    return pl.pallas_call(
        functools.partial(choose_kernel, n, n_tp, steps),
        out_shape=[jax.ShapeDtypeStruct((n // n_tp, half, wide), jnp.bfloat16)] * 2,
        in_specs=[vmem] * 4,
        out_specs=[vmem, vmem],
        compiler_params=params,
        name="choose",
    )(*arrays)


def join_kernel(mine_ref, got_ref, out_ref):
    odd = lax.axis_index("tp") % 2
    count, half, _ = mine_ref.shape
    for low in range(2):
        first, second = (mine_ref, got_ref) if low == 0 else (got_ref, mine_ref)

        @pl.when(odd == low)
        def _():
            for i in range(count):
                out_ref[2 * i * half : (2 * i + 1) * half] = first[i]
                out_ref[(2 * i + 1) * half : (2 * i + 2) * half] = second[i]


def join(mine, got):
    count, half, wide = mine.shape
    return pl.pallas_call(
        join_kernel,
        out_shape=jax.ShapeDtypeStruct((2 * count * half, wide), jnp.bfloat16),
        in_specs=[vmem, vmem],
        out_specs=vmem,
        compiler_params=params,
        name="join",
    )(mine, got)


def after(array, token):
    return lax.optimization_barrier((array, token))[0]


def body(n, n_tp, queries, suffix_kv, cache_pool, hit_count, hit_slots, out_weight):
    tok = queries.shape[0]
    half = n // 2
    order = ring_order(n)
    right = [(order[i], order[(i + 1) % n]) for i in range(n)]
    left = [(b, a) for a, b in right]

    def send_both(pair, k, token):
        from_left, from_right = pair
        if token is not None:
            from_left = after(from_left, token)
            from_right = after(from_right, token)
        return lax.ppermute(from_left, "ctx", right), lax.ppermute(from_right, "ctx", left)

    def ring(own, visit, token):
        held = [send_both((a, a), k, None) for k, a in enumerate(own)]
        for step in range(1, half):
            token = visit(step - 1, arrived if step > 1 else None, token)
            arrived = held
            if step < half - 1:
                held = [send_both(arrived[k], k, token) for k in range(2)]
            else:
                held = (
                    lax.ppermute(after(arrived[0][0], token), "ctx", right),
                    lax.ppermute(after(arrived[1][1], token), "ctx", left),
                )
        token = visit(half - 1, arrived, token)
        return held, token

    def absorb(step, arrived, state):
        if step == 0:
            return flash(n, tok, queries, hit_count, ((0, 0), (1, 0)), own, (), False)
        turned, state = state[0], state[1:]
        for kind in range(2):
            pieces = ((kind, -step), (kind, step))
            state = flash(n, tok, turned, hit_count, pieces, arrived[kind], state, False)
        return [turned] + list(state)

    own = pick(hit_slots, cache_pool, suffix_kv)
    far, state = ring(own, absorb, None)
    attention = flash(
        n, tok, state[0], hit_count, ((0, half), (1, half)), far, tuple(state[1:]), True
    )

    swap = [(t, t ^ 1) for t in range(n_tp)]
    sums = []

    def reduce(arrays):
        keep, send = project(arrays, out_weight)
        sums.append((keep, lax.ppermute(send, "tp", swap)))
        return send

    def spread(step, arrived, token):
        if step == 0:
            return attention[0]
        (a_left, a_right), (b_left, b_right) = arrived
        arrays = (a_left, b_left, a_right, b_right)
        return reduce(tuple(attention) + arrays if step == 1 else arrays)

    def cross(stay, send):
        got = lax.ppermute(send, "tp", [(t, t ^ 2) for t in range(n_tp)])
        bit = 4
        while bit < n_tp:
            stay = added(stay, got).astype(jnp.bfloat16)
            got = lax.ppermute(stay, "tp", [(t, t ^ bit) for t in range(n_tp)])
            bit *= 2
        return stay, got

    far, _ = ring(attention, spread, None)
    steps = [0] + [s * d for d in range(1, half) for s in (-1, 1)] + [half]
    sums[0] = (after(sums[0][0], far), sums[0][1])
    stay, send, last_stay, last_send = sort(n, n_tp, steps[:-1], sums)
    stay, got = cross(stay, send)
    reduce(far)
    last_stay, last_send = place_last(n, n_tp, *sums[-1], last_stay, last_send)
    last_stay, last_got = cross(last_stay, last_send)
    mine, give = choose(n, n_tp, steps, (stay, got, last_stay, last_got))
    return join(mine, lax.ppermute(give, "tp", swap))


def solution(mesh):
    n, n_tp = mesh.shape["ctx"], mesh.shape["tp"]
    placed = (
        P("ctx", "tp"),
        P(None, "ctx", "tp"),
        P(None, "ctx", None, "tp"),
        P(),
        P("ctx", None),
        P("tp", "ctx"),
    )
    return jax.shard_map(
        functools.partial(body, n, n_tp),
        mesh=mesh,
        in_specs=placed,
        out_specs=P("tp", "ctx"),
        check_vma=False,
    )
```

```python
import functools
import math

import jax
import jax.numpy as jnp
from jax import lax
from jax.experimental import pallas as pl
from jax.experimental.pallas import tpu as pltpu
from jax.sharding import PartitionSpec as P

HD = 128
HCAP = 3
neg_fill = -1e30
score_scale = 1.0 / math.sqrt(HD)
kernel_vmem = 16 * 1024 * 1024

vmem = pl.BlockSpec(memory_space=pltpu.VMEM)
smem = pl.BlockSpec(memory_space=pltpu.SMEM)
hbm = pl.BlockSpec(memory_space=pltpu.HBM)
params = pltpu.CompilerParams(vmem_limit_bytes=kernel_vmem)
light = pl.CostEstimate(flops=1000, bytes_accessed=1000, transcendentals=0)


def ring_order(n):
    return [2 * q if 2 * q < n else 2 * (n - 1 - q) + 1 for q in range(n)]


def owner_of(me, step, n):
    place = jnp.where(me % 2 == 0, me // 2, n - 1 - me // 2)
    place = lax.rem(place + step + n, n)
    return jnp.where(2 * place < n, 2 * place, 2 * (n - 1 - place) + 1)


def pick_kernel(blk, hit_slots, pool_ref, suffix_ref, near_ref, rest_ref, held, slots_ref, slots_sem, sems):
    outs = (near_ref, rest_ref)
    fetch = pltpu.make_async_copy(hit_slots, slots_ref, slots_sem)
    fetch.start()
    fetch.wait()
    copies = []
    for kv in range(2):
        for place in range(HCAP + 1):
            if place == 0:
                src = suffix_ref.at[kv]
            else:
                src = pool_ref.at[kv, slots_ref[0, place - 1]]
            if kv == 0:
                dst = outs[place // 2].at[0, pl.ds(place % 2 * blk, blk), :]
            else:
                dst = held.at[place]
            copies.append(pltpu.make_async_copy(src, dst, sems.at[kv, place]))
    for copy in copies:
        copy.start()
    for copy in copies:
        copy.wait()
    for place in range(HCAP + 1):
        for lane in range(0, held.shape[2], HD):
            at = slice(place % 2 * blk, (place % 2 + 1) * blk)
            outs[place // 2][1, at, lane : lane + HD] = held[place, :, lane : lane + HD].T


def pick(hit_slots, cache_pool, suffix_kv):
    blk, wide = cache_pool.shape[2:]
    return pl.pallas_call(
        functools.partial(pick_kernel, blk),
        out_shape=[jax.ShapeDtypeStruct((2, 2 * blk, wide), jnp.bfloat16)] * 2,
        in_specs=[hbm, hbm, hbm],
        out_specs=[vmem, vmem],
        scratch_shapes=[
            pltpu.VMEM((HCAP + 1, blk, wide), jnp.bfloat16),
            pltpu.SMEM(hit_slots.shape, jnp.int32),
            pltpu.SemaphoreType.DMA,
            pltpu.SemaphoreType.DMA((2, HCAP + 1)),
        ],
        compiler_params=pltpu.CompilerParams(vmem_limit_bytes=60 * 1024 * 1024),
        name="pick",
    )(hit_slots, cache_pool, suffix_kv)


def fold(op, array):
    parts = [array[r : r + 8] for r in range(0, array.shape[0], 8)]
    while len(parts) > 1:
        pairs = [op(a, b) for a, b in zip(parts[::2], parts[1::2])]
        parts = pairs + parts[len(parts) - len(parts) % 2 :]
    return parts[0]


def flash_kernel(n, tok, pieces, first, last, hit_ref, q_ref, *refs):
    count = len(pieces)
    kv_refs, refs = refs[:count], refs[count:]
    me = lax.axis_index("ctx")
    heads = (q_ref.shape[1] if first else q_ref.shape[1] // tok * HD) // HD
    keys, wide = kv_refs[0].shape[1:]
    blk = keys // 2
    slots_dev = wide // HD
    group = heads // slots_dev
    per = 2 if group % 2 == 0 else 1
    rows = per * tok
    biases = []
    for kind, step in pieces:
        owner = owner_of(me, step, n)
        if kind == 0:
            seen = [None if step == 0 else owner < me, None]
        else:
            seen = [hit_ref[owner] > 1, hit_ref[owner] > 2]
        biases.append([0.0 if s is None else jnp.where(s, 0.0, neg_fill) for s in seen])

    def place(j):
        head = j * per
        cols = [slice((head + h) * HD, (head + h + 1) * HD) for h in range(per)]
        slot = head // group
        return cols, slice(head * tok, head * tok + rows), slice(slot * HD, (slot + 1) * HD)

    def score(j):
        cols, at, lanes = place(j)
        if first:
            turned = jnp.concatenate([q_ref[:, c].T for c in cols], axis=1)
            refs[-4][:, at] = turned
        else:
            turned = q_ref[:, at]
        scores = []
        for (kind, step), ref, bias in zip(pieces, kv_refs, biases):
            raw = jnp.dot(ref[0, :, lanes], turned, preferred_element_type=jnp.float32)
            for b in range(2):
                part = raw[b * blk : (b + 1) * blk]
                if (kind, step, b) == (0, 0, 0):
                    key = lax.broadcasted_iota(jnp.int32, part.shape, 0)
                    token = lax.broadcasted_iota(jnp.int32, part.shape, 1) % tok
                    part = jnp.where(key <= token, part, neg_fill)
                scores.append((part, bias[b]))
        return scores

    def weigh(j, scores):
        _, at, _ = place(j)
        tops = [fold(jnp.maximum, part) + bias for part, bias in scores]
        top = jnp.max(functools.reduce(jnp.maximum, tops), axis=0, keepdims=True)
        total = fade = None
        if not first:
            m_in, l_in, _ = refs[:3]
            old_top = m_in[:, at]
            top = jnp.maximum(old_top, top)
            fade = jnp.exp((old_top - top) * score_scale)
            total = l_in[:, at] * fade
        if not last:
            refs[-3][:, at] = jnp.broadcast_to(top, (8, rows))
        offset = top[:1] * score_scale
        probs = []
        for part, bias in scores:
            weights = jnp.exp(part * score_scale - (offset - bias))
            add = fold(jnp.add, weights)
            total = add if total is None else total + add
            probs.append(weights.astype(jnp.bfloat16))
        if not last:
            refs[-2][:, at] = total
        return jnp.concatenate(probs, axis=0), fade, total

    def mix(j, probs, fade, total):
        cols, at, lanes = place(j)
        values = [ref[1, b * blk : (b + 1) * blk, lanes] for ref in kv_refs for b in range(2)]
        mixed = jnp.dot(
            jnp.concatenate(values, axis=1), probs, preferred_element_type=jnp.float32
        )
        if not first:
            mixed = mixed + refs[2][:, at] * fade[:1]
        if not last:
            refs[-1][:, at] = mixed
            return
        result = mixed * (1.0 / jnp.sum(total, axis=0, keepdims=True))
        half = tok // 2
        for h, c in enumerate(cols):
            head_out = result[:, h * tok : (h + 1) * tok].T.astype(jnp.bfloat16)
            for k, out in enumerate(refs[-2:]):
                out[:, c] = head_out[k * half : (k + 1) * half]

    blocks = heads // per
    ahead = min(2, blocks)
    scores = [score(j) for j in range(ahead)]
    for j in range(blocks):
        weighed = weigh(j, scores[j])
        scores[j] = None
        if j + ahead < blocks:
            scores.append(score(j + ahead))
        mix(j, *weighed)


def flash(n, tok, queries, hit_count, pieces, arrays, state, last):
    rows = queries.size // HD
    small = jax.ShapeDtypeStruct((8, rows), jnp.float32)
    if last:
        out_shape = [jax.ShapeDtypeStruct((tok // 2, rows // tok * HD), jnp.bfloat16)] * 2
        aliases = {}
    else:
        out_shape = [small, small, jax.ShapeDtypeStruct((HD, rows), jnp.float32)]
        aliases = {2 + len(arrays) + i: i for i in range(len(state))}
    if not state:
        out_shape = [jax.ShapeDtypeStruct((HD, rows), jnp.bfloat16)] + out_shape
    return pl.pallas_call(
        functools.partial(flash_kernel, n, tok, pieces, not state, last),
        out_shape=out_shape,
        in_specs=[smem] + [vmem] * (1 + len(arrays) + len(state)),
        out_specs=[vmem] * len(out_shape),
        input_output_aliases=aliases,
        compiler_params=params,
        cost_estimate=light,
        name="flash",
    )(hit_count, queries, *arrays, *state)


def project_kernel(count, *refs):
    shard_refs, (w_ref, keep_ref, send_ref) = refs[: 2 * count], refs[2 * count :]
    odd = lax.axis_index("tp") % 2
    rows = jnp.concatenate([ref[...] for ref in shard_refs], axis=0)
    half = rows.shape[0] // (2 * count)
    wide = w_ref.shape[1]
    width = min(256, wide)
    for col in range(0, wide, width):
        at = slice(col, col + width)
        product = jnp.dot(rows, w_ref[:, at], preferred_element_type=jnp.float32)
        product = product.astype(jnp.bfloat16)
        for i in range(count):
            low = product[2 * i * half : (2 * i + 1) * half]
            high = product[(2 * i + 1) * half : (2 * i + 2) * half]

            @pl.when(odd == 0)
            def _():
                keep_ref[i, :, at] = low
                send_ref[i, :, at] = high

            @pl.when(odd == 1)
            def _():
                keep_ref[i, :, at] = high
                send_ref[i, :, at] = low


def project(arrays, out_weight):
    half = arrays[0].shape[0]
    depth, wide = out_weight.shape
    count = len(arrays) // 2
    return pl.pallas_call(
        functools.partial(project_kernel, count),
        out_shape=[jax.ShapeDtypeStruct((count, half, wide), jnp.bfloat16)] * 2,
        in_specs=[vmem] * (len(arrays) + 1),
        out_specs=[vmem, vmem],
        compiler_params=params,
        cost_estimate=light,
        name="project",
    )(*arrays, out_weight)


def sides(n, n_tp, steps):
    me = lax.axis_index("ctx")
    my_tp = lax.axis_index("tp")
    share = n // n_tp
    found, near_count, away_count = [], jnp.int32(0), jnp.int32(0)
    for step in steps:
        owner = owner_of(me, step, n)
        away = lax.bitwise_xor(owner // share, my_tp) // 2 % 2
        found.append((owner, away, jnp.where(away == 1, away_count, near_count)))
        near_count = near_count + 1 - away
        away_count = away_count + away
    return found


def added(a, b):
    return a.astype(jnp.float32) + b.astype(jnp.float32)


def sort_kernel(n, n_tp, steps, *refs):
    *refs, stay_ref, send_ref, last_stay_ref, last_send_ref = refs
    count = len(refs) // 2
    places = [(a, b, i) for a, b in zip(refs[:count], refs[count:]) for i in range(a.shape[0])]
    full = stay_ref.shape[0]
    for (a, b, i), (_, away, rank) in zip(places, sides(n, n_tp, steps)):
        total = added(a[i], b[i]).astype(jnp.bfloat16)
        for side, out, last in ((0, stay_ref, last_stay_ref), (1, send_ref, last_send_ref)):

            @pl.when((away == side) & (rank < full))
            def _():
                out[rank] = total

            @pl.when((away == side) & (rank == full))
            def _():
                last[0] = total


def sort(n, n_tp, steps, sums):
    keeps, gots = zip(*sums)
    half, wide = keeps[0].shape[1:]
    many = jax.ShapeDtypeStruct((n // 2 - 1, half, wide), jnp.bfloat16)
    one = jax.ShapeDtypeStruct((1, half, wide), jnp.bfloat16)
    return pl.pallas_call(
        functools.partial(sort_kernel, n, n_tp, steps),
        out_shape=[many, many, one, one],
        in_specs=[vmem] * (2 * len(sums)),
        out_specs=[vmem] * 4,
        compiler_params=params,
        cost_estimate=light,
        name="sort",
    )(*keeps, *gots)


def last_kernel(n, n_tp, keep_ref, got_ref, stay_in, send_in, stay_ref, send_ref):
    ((_, away, _),) = sides(n, n_tp, (n // 2,))
    total = added(keep_ref[...], got_ref[...]).astype(jnp.bfloat16)
    stay_ref[...] = jnp.where(away == 0, total, stay_in[...])
    send_ref[...] = jnp.where(away == 1, total, send_in[...])


def place_last(n, n_tp, keep, got, stay, send):
    return pl.pallas_call(
        functools.partial(last_kernel, n, n_tp),
        out_shape=[jax.ShapeDtypeStruct(keep.shape, jnp.bfloat16)] * 2,
        in_specs=[vmem] * 4,
        out_specs=[vmem] * 2,
        compiler_params=params,
        cost_estimate=light,
        name="last",
    )(keep, got, stay, send)


def choose_kernel(n, n_tp, steps, *refs):
    stay, got, last_stay, last_got, mine_ref, give_ref = refs
    my_tp = lax.axis_index("tp")
    share = n // n_tp
    found = sides(n, n_tp, steps)
    full = stay.shape[0]
    for r in range(full + 1):
        owner = jnp.int32(0)
        for candidate, away, rank in found:
            owner = jnp.where((away == 0) & (rank == r), candidate, owner)
        if r < full:
            total = added(stay[r], got[r])
        else:
            total = added(last_stay[0], last_got[0])
        for out, block in ((mine_ref, my_tp), (give_ref, lax.bitwise_xor(my_tp, 1))):

            @pl.when(owner // share == block)
            def _():
                out[owner % share] = total.astype(out.dtype)


def choose(n, n_tp, steps, arrays):
    half, wide = arrays[0].shape[1:]
    return pl.pallas_call(
        functools.partial(choose_kernel, n, n_tp, steps),
        out_shape=[jax.ShapeDtypeStruct((n // n_tp, half, wide), jnp.bfloat16)] * 2,
        in_specs=[vmem] * 4,
        out_specs=[vmem, vmem],
        compiler_params=params,
        name="choose",
    )(*arrays)


def join_kernel(mine_ref, got_ref, out_ref):
    odd = lax.axis_index("tp") % 2
    count, half, _ = mine_ref.shape
    for low in range(2):
        first, second = (mine_ref, got_ref) if low == 0 else (got_ref, mine_ref)

        @pl.when(odd == low)
        def _():
            for i in range(count):
                out_ref[2 * i * half : (2 * i + 1) * half] = first[i]
                out_ref[(2 * i + 1) * half : (2 * i + 2) * half] = second[i]


def join(mine, got):
    count, half, wide = mine.shape
    return pl.pallas_call(
        join_kernel,
        out_shape=jax.ShapeDtypeStruct((2 * count * half, wide), jnp.bfloat16),
        in_specs=[vmem, vmem],
        out_specs=vmem,
        compiler_params=params,
        name="join",
    )(mine, got)


def after(array, token):
    return lax.optimization_barrier((array, token))[0]


def body(n, n_tp, queries, suffix_kv, cache_pool, hit_count, hit_slots, out_weight):
    tok = queries.shape[0]
    half = n // 2
    order = ring_order(n)
    right = [(order[i], order[(i + 1) % n]) for i in range(n)]
    left = [(b, a) for a, b in right]

    def send_both(pair, k, token):
        from_left, from_right = pair
        if token is not None:
            from_left = after(from_left, token)
            from_right = after(from_right, token)
        return lax.ppermute(from_left, "ctx", right), lax.ppermute(from_right, "ctx", left)

    def ring(own, visit, token):
        held = [send_both((a, a), k, None) for k, a in enumerate(own)]
        for step in range(1, half):
            token = visit(step - 1, arrived if step > 1 else None, token)
            arrived = held
            if step < half - 1:
                held = [send_both(arrived[k], k, token) for k in range(2)]
            else:
                held = (
                    lax.ppermute(after(arrived[0][0], token), "ctx", right),
                    lax.ppermute(after(arrived[1][1], token), "ctx", left),
                )
        token = visit(half - 1, arrived, token)
        return held, token

    def absorb(step, arrived, state):
        if step == 0:
            return flash(n, tok, queries, hit_count, ((0, 0), (1, 0)), own, (), False)
        turned, state = state[0], state[1:]
        for kind in range(2):
            pieces = ((kind, -step), (kind, step))
            state = flash(n, tok, turned, hit_count, pieces, arrived[kind], state, False)
        return [turned] + list(state)

    own = pick(hit_slots, cache_pool, suffix_kv)
    far, state = ring(own, absorb, None)
    attention = flash(
        n, tok, state[0], hit_count, ((0, half), (1, half)), far, tuple(state[1:]), True
    )

    swap = [(t, t ^ 1) for t in range(n_tp)]
    sums = []

    def reduce(arrays):
        keep, send = project(arrays, out_weight)
        sums.append((keep, lax.ppermute(send, "tp", swap)))
        return send

    def spread(step, arrived, token):
        if step == 0:
            return attention[0]
        (a_left, a_right), (b_left, b_right) = arrived
        arrays = (a_left, b_left, a_right, b_right)
        return reduce(tuple(attention) + arrays if step == 1 else arrays)

    def cross(stay, send):
        got = lax.ppermute(send, "tp", [(t, t ^ 2) for t in range(n_tp)])
        bit = 4
        while bit < n_tp:
            stay = added(stay, got).astype(jnp.bfloat16)
            got = lax.ppermute(stay, "tp", [(t, t ^ bit) for t in range(n_tp)])
            bit *= 2
        return stay, got

    far, _ = ring(attention, spread, None)
    steps = [0] + [s * d for d in range(1, half) for s in (-1, 1)] + [half]
    sums[0] = (after(sums[0][0], far), sums[0][1])
    stay, send, last_stay, last_send = sort(n, n_tp, steps[:-1], sums)
    stay, got = cross(stay, send)
    reduce(far)
    last_stay, last_send = place_last(n, n_tp, *sums[-1], last_stay, last_send)
    last_stay, last_got = cross(last_stay, last_send)
    mine, give = choose(n, n_tp, steps, (stay, got, last_stay, last_got))
    return join(mine, lax.ppermute(give, "tp", swap))


def pair_pick_kernel(blk, hit_slots, pool_ref, suffix_ref, mine_ref, other_ref, held, slots_ref, slots_sem, sems):
    fetch = pltpu.make_async_copy(hit_slots, slots_ref, slots_sem)
    fetch.start()
    fetch.wait()
    copies = []
    for kv in range(2):
        for place in range(HCAP + 1):
            if place == 0:
                src = suffix_ref.at[kv]
            else:
                src = pool_ref.at[kv, slots_ref[0, place - 1]]
            copies.append(pltpu.make_async_copy(src, held.at[kv, place], sems.at[kv, place]))
    for copy in copies:
        copy.start()
    for copy in copies:
        copy.wait()
    parity = lax.axis_index("ctx") % 2
    for place in range(HCAP + 1):
        at = slice(place * blk, (place + 1) * blk)
        keys = [held[0, place, :, s * HD : (s + 1) * HD] for s in range(2)]
        values = [held[1, place, :, s * HD : (s + 1) * HD].T for s in range(2)]
        mine_ref[0, at, :] = jnp.where(parity == 0, keys[0], keys[1])
        mine_ref[1, at, :] = jnp.where(parity == 0, values[0], values[1])
        other_ref[0, at, :] = jnp.where(parity == 0, keys[1], keys[0])
        other_ref[1, at, :] = jnp.where(parity == 0, values[1], values[0])


def pair_pick(hit_slots, cache_pool, suffix_kv):
    blk, wide = cache_pool.shape[2:]
    return pl.pallas_call(
        functools.partial(pair_pick_kernel, blk),
        out_shape=[jax.ShapeDtypeStruct((2, (HCAP + 1) * blk, HD), jnp.bfloat16)] * 2,
        in_specs=[hbm, hbm, hbm],
        out_specs=[vmem, vmem],
        scratch_shapes=[
            pltpu.VMEM((2, HCAP + 1, blk, wide), jnp.bfloat16),
            pltpu.SMEM(hit_slots.shape, jnp.int32),
            pltpu.SemaphoreType.DMA,
            pltpu.SemaphoreType.DMA((2, HCAP + 1)),
        ],
        compiler_params=pltpu.CompilerParams(vmem_limit_bytes=60 * 1024 * 1024),
        name="pick",
    )(hit_slots, cache_pool, suffix_kv)


def attend(blocks, score, biases, values, old, store):
    def weigh(j, scores):
        tops = [fold(jnp.maximum, part) + bias for part, bias in zip(scores, biases)]
        top = jnp.max(functools.reduce(jnp.maximum, tops), axis=0, keepdims=True)
        total = fade = mixed = None
        if old is not None:
            old_top, old_total, old_mixed = old(j)
            top = jnp.maximum(old_top, top)
            fade = jnp.exp((old_top - top) * score_scale)
            total, mixed = old_total * fade, old_mixed
        else:
            top = jnp.broadcast_to(top, (8, top.shape[1]))
        offset = top[:1] * score_scale
        probs = []
        for part, bias in zip(scores, biases):
            weights = jnp.exp(part * score_scale - (offset - bias))
            add = fold(jnp.add, weights)
            total = add if total is None else total + add
            probs.append(weights.astype(jnp.bfloat16))
        return jnp.concatenate(probs, axis=0), top, total, fade, mixed

    def mix(j, probs, top, total, fade, mixed):
        add = jnp.dot(values, probs, preferred_element_type=jnp.float32)
        store(j, top, total, add if mixed is None else mixed * fade[:1] + add)

    ahead = min(2, blocks)
    scores = [score(j) for j in range(ahead)]
    for j in range(blocks):
        weighed = weigh(j, scores[j])
        scores[j] = None
        if j + ahead < blocks:
            scores.append(score(j + ahead))
        mix(j, *weighed)


def squares(values, blk):
    return jnp.concatenate(
        [values[r : r + blk] for r in range(0, values.shape[0], blk)], axis=1
    )


def hit_biases(hits, suffix_seen):
    seen = [suffix_seen, None] + [hits > h for h in range(1, HCAP)]
    return [0.0 if s is None else jnp.where(s, 0.0, neg_fill) for s in seen]


def causal(parts, owner, tok):
    key = lax.broadcasted_iota(jnp.int32, parts[0].shape, 0) + owner % 2 * tok
    token = lax.broadcasted_iota(jnp.int32, parts[0].shape, 1)
    return [jnp.where(key <= token, parts[0], neg_fill)] + parts[1:]


def pair_first_kernel(tok, hit_ref, q_ref, q_got_ref, mine_ref, turned_ref, *state):
    me = lax.axis_index("ctx")
    parity = me % 2
    heads = q_got_ref.shape[1] // HD
    rows = 2 * tok
    blk = tok
    biases = hit_biases(hit_ref[me], None)
    values = squares(mine_ref[1], blk)

    def score(j):
        own = q_ref[:, pl.ds(pl.multiple_of((parity * heads + j) * HD, HD), HD)].T
        got = q_got_ref[:, j * HD : (j + 1) * HD].T
        low = jnp.where(parity == 0, own, got)
        high = jnp.where(parity == 0, got, own)
        turned = jnp.concatenate([low, high], axis=1)
        turned_ref[:, j * rows : (j + 1) * rows] = turned
        raw = jnp.dot(mine_ref[0], turned, preferred_element_type=jnp.float32)
        return causal([raw[r : r + blk] for r in range(0, raw.shape[0], blk)], me, tok)

    def store(j, *new):
        for ref, array in zip(state, new):
            ref[:, j * rows : (j + 1) * rows] = array

    attend(heads, score, biases, values, None, store)


def pair_step_kernel(n, tok, step, part, last, hit_ref, turned_ref, left_ref, right_ref, *refs):
    old_refs, out_refs = refs[:3], refs[3:]
    me = lax.axis_index("ctx")
    level, levels = me // 2, n // 2
    home = lax.bitwise_xor(me, part)
    rows = 2 * tok
    blk = tok
    heads = turned_ref.shape[1] // rows
    reach = jnp.where(me % 2 == 0, step, -step)
    from_left = (level - reach >= 0) & (level - reach < levels)
    from_right = (level + reach >= 0) & (level + reach < levels)

    def at(j):
        return slice(j * rows, (j + 1) * rows)

    def old(j):
        return tuple(ref[:, at(j)] for ref in old_refs)

    def store(j, top, total, mixed):
        if last:
            result = mixed * (1.0 / jnp.sum(total, axis=0, keepdims=True))
            for k, out in enumerate(out_refs):
                square = result[:, k * tok : (k + 1) * tok]
                out[:, j * HD : (j + 1) * HD] = square.T.astype(jnp.bfloat16)
        else:
            for ref, array in zip(out_refs, (top, total, mixed)):
                ref[:, at(j)] = array

    def run(keys, values, biases):
        def score(j):
            scores = []
            for block in keys:
                raw = jnp.dot(block, turned_ref[:, at(j)], preferred_element_type=jnp.float32)
                scores += [raw[r : r + blk] for r in range(0, raw.shape[0], blk)]
            return causal(scores, home, tok) if step == 0 else scores

        attend(heads, score, biases, values, old, store)

    if step == 0:
        run([left_ref[0]], squares(left_ref[1], blk), hit_biases(hit_ref[home], None))
        return

    @pl.when(from_left != from_right)
    def _():
        keys = jnp.where(from_left, left_ref[0], right_ref[0])
        values = jnp.where(from_left, left_ref[1], right_ref[1])
        owner = home - 2 * jnp.where(from_left, reach, -reach)
        run([keys], squares(values, blk), hit_biases(hit_ref[owner], owner < home))

    if 2 * step < levels:

        @pl.when(from_left & from_right)
        def _():
            values = [squares(ref[1], blk) for ref in (left_ref, right_ref)]
            biases = hit_biases(hit_ref[home - 2 * reach], reach > 0)
            biases += hit_biases(hit_ref[home + 2 * reach], reach < 0)
            run([left_ref[0], right_ref[0]], jnp.concatenate(values, axis=1), biases)

    if 2 * step > levels:

        @pl.when(jnp.logical_not(from_left | from_right))
        def _():
            for j in range(heads):
                store(j, *old(j))


def pair_flash(kernel, tok, rows, operands, states, last):
    small = jax.ShapeDtypeStruct((8, rows), jnp.float32)
    shapes = [small, small, jax.ShapeDtypeStruct((HD, rows), jnp.float32)]
    aliases = {len(operands) + i: i for i in range(len(states))}
    if not states:
        shapes = [jax.ShapeDtypeStruct((HD, rows), jnp.bfloat16)] + shapes
    if last:
        shapes = [jax.ShapeDtypeStruct((tok, rows // (2 * tok) * HD), jnp.bfloat16)] * 2
        aliases = {}
    return pl.pallas_call(
        kernel,
        out_shape=shapes,
        in_specs=[smem] + [vmem] * (len(operands) - 1 + len(states)),
        out_specs=[vmem] * len(shapes),
        input_output_aliases=aliases,
        compiler_params=params,
        cost_estimate=light,
        name="flash",
    )(*operands, *states)


def times_weight(me, step, n, low, high, w_ref, at):
    depth = w_ref.shape[0] // 2
    owner = owner_of(me, step, n)
    rows = jnp.concatenate([low[...], high[...]], axis=0)
    side = w_ref[pl.ds(pl.multiple_of(owner % 2 * depth, depth), depth), at]
    return owner, jnp.dot(rows, side, preferred_element_type=jnp.float32)


def pair_project_kernel(n, steps, *refs):
    arrays, w_ref, out_ref = refs[: 2 * len(steps)], refs[2 * len(steps)], refs[-1]
    me = lax.axis_index("ctx")
    wide = w_ref.shape[1]
    width = min(256, wide)
    for col in range(0, wide, width):
        at = slice(col, col + width)
        for i, step in enumerate(steps):
            owner, product = times_weight(
                me, step, n, arrays[2 * i], arrays[2 * i + 1], w_ref, at
            )
            out_ref[owner, :, at] = product.astype(jnp.bfloat16)


def pair_project(n, steps, arrays, out_weight, buffer):
    shape = (n, 2 * arrays[0].shape[0], out_weight.shape[1])
    return pl.pallas_call(
        functools.partial(pair_project_kernel, n, steps),
        out_shape=jax.ShapeDtypeStruct(shape, jnp.bfloat16),
        in_specs=[vmem] * (len(arrays) + 1 + len(buffer)),
        out_specs=vmem,
        input_output_aliases={len(arrays) + 1: 0} if buffer else {},
        compiler_params=params,
        cost_estimate=light,
        name="project",
    )(*arrays, out_weight, *buffer)


def levels_of(n):
    me = lax.axis_index("ctx")
    side = lax.axis_index("tp") // 2
    far = owner_of(me, n // 2, n) // 2
    stay = jnp.where(far == 2 * side, 2 * side + 1, 2 * side)
    away = 2 * (1 - side)
    send = jnp.where(far == away, away + 1, away)
    other = jnp.where(far // 2 == side, away + 1, 2 * side + 1)
    return stay, send, other, far


def split_halves(total, keep, send, i, at):
    odd = lax.axis_index("tp") % 2
    half = total.shape[0] // 2
    low, high = total[:half], total[half:]
    keep[i, :, at] = jnp.where(odd == 0, low, high).astype(jnp.bfloat16)
    send[i, :, at] = jnp.where(odd == 0, high, low).astype(jnp.bfloat16)


def pair_add_kernel(n, buffer_ref, keep_ref, *send_refs):
    odd = lax.axis_index("tp") % 2
    pieces = len(send_refs) // 3
    for i, level in enumerate(levels_of(n)[:3]):
        total = added(buffer_ref[2 * level], buffer_ref[2 * level + 1]).astype(jnp.bfloat16)
        half = total.shape[0] // 2
        size = half // pieces
        low, high = total[:half], total[half:]
        keep_ref[i] = jnp.where(odd == 0, low, high)
        send = jnp.where(odd == 0, high, low)
        for k in range(pieces):
            send_refs[i * pieces + k][0] = send[k * size : (k + 1) * size]


def pair_add(n, buffer, pieces=2):
    _, rows, wide = buffer.shape
    return pl.pallas_call(
        functools.partial(pair_add_kernel, n),
        out_shape=[jax.ShapeDtypeStruct((3, rows // 2, wide), jnp.bfloat16)]
        + [jax.ShapeDtypeStruct((1, rows // 2 // pieces, wide), jnp.bfloat16)] * (3 * pieces),
        in_specs=[vmem],
        out_specs=[vmem] * (1 + 3 * pieces),
        compiler_params=params,
        cost_estimate=light,
        name="add",
    )(buffer)


def pair_far_kernel(n, low, high, w_ref, buffer_ref, keep_ref, send_ref):
    me = lax.axis_index("ctx")
    wide = w_ref.shape[1]
    width = min(256, wide)
    for col in range(0, wide, width):
        at = slice(col, col + width)
        owner, product = times_weight(me, n // 2, n, low, high, w_ref, at)
        total = product + buffer_ref[lax.bitwise_xor(owner, 1), :, at].astype(jnp.float32)
        split_halves(total, keep_ref, send_ref, 0, at)


def pair_far(n, arrays, out_weight, buffer):
    _, rows, wide = buffer.shape
    return pl.pallas_call(
        functools.partial(pair_far_kernel, n),
        out_shape=[jax.ShapeDtypeStruct((1, rows // 2, wide), jnp.bfloat16)] * 2,
        in_specs=[vmem] * 4,
        out_specs=[vmem, vmem],
        compiler_params=params,
        cost_estimate=light,
        name="project",
    )(*arrays, out_weight, buffer)


def pair_sort_kernel(keep_ref, *refs):
    got_refs, outs = refs[:-3], refs[-3:]
    pieces = len(got_refs) // 3
    size = keep_ref.shape[1] // pieces
    for i, out in enumerate(outs):
        for k in range(pieces):
            at = slice(k * size, (k + 1) * size)
            got = got_refs[i * pieces + k][0]
            out[0, at, :] = added(keep_ref[i, at, :], got).astype(jnp.bfloat16)


def pair_sort(keep, got):
    shape = jax.ShapeDtypeStruct((1,) + keep.shape[1:], jnp.bfloat16)
    return pl.pallas_call(
        pair_sort_kernel,
        out_shape=[shape] * 3,
        in_specs=[vmem] * (1 + len(got)),
        out_specs=[vmem] * 3,
        compiler_params=params,
        cost_estimate=light,
        name="sort",
    )(keep, *got)


def pair_last_kernel(n, keep_ref, got_ref, other_ref, stay_ref, send_ref):
    far = levels_of(n)[3]
    stays = far // 2 == lax.axis_index("tp") // 2
    total = added(keep_ref[...], got_ref[...]).astype(jnp.bfloat16)
    stay_ref[...] = jnp.where(stays, total, other_ref[...])
    send_ref[...] = jnp.where(stays, other_ref[...], total)


def pair_last(n, keep, got, other):
    return pl.pallas_call(
        functools.partial(pair_last_kernel, n),
        out_shape=[jax.ShapeDtypeStruct(keep.shape, jnp.bfloat16)] * 2,
        in_specs=[vmem] * 3,
        out_specs=[vmem] * 2,
        compiler_params=params,
        cost_estimate=light,
        name="last",
    )(keep, got, other)


def pair_choose_kernel(n, stay_ref, got_ref, last_stay_ref, last_got_ref, mine_ref, give_ref):
    first = levels_of(n)[0] == lax.axis_index("tp")
    early = added(stay_ref[...], got_ref[...]).astype(jnp.bfloat16)
    late = added(last_stay_ref[...], last_got_ref[...]).astype(jnp.bfloat16)
    mine_ref[...] = jnp.where(first, early, late)
    give_ref[...] = jnp.where(first, late, early)


def pair_choose(n, *arrays):
    return pl.pallas_call(
        functools.partial(pair_choose_kernel, n),
        out_shape=[jax.ShapeDtypeStruct(arrays[0].shape, jnp.bfloat16)] * 2,
        in_specs=[vmem] * 4,
        out_specs=[vmem, vmem],
        compiler_params=params,
        cost_estimate=light,
        name="choose",
    )(*arrays)


def pair_body(n, n_tp, queries, suffix_kv, cache_pool, hit_count, hit_slots, out_weight):
    tok, wide = queries.shape
    half, levels = n // 2, n // 2
    order = ring_order(n)
    right = [(order[i], order[(i + 1) % n]) for i in range(n)]
    left = [(b, a) for a, b in right]
    swap = [(t, t ^ 1) for t in range(n_tp)]
    over = [(t, t ^ 2) for t in range(n_tp)]
    flip = [(i, i ^ 1) for i in range(n)]
    parity = lax.axis_index("ctx") % 2

    def both(pair, ways, token):
        if token is not None:
            pair = [after(a, token) for a in pair]
        return tuple(lax.ppermute(a, "ctx", way) for a, way in zip(pair, ways))

    mine, other = pair_pick(hit_slots, cache_pool, suffix_kv)
    near = [both((mine, mine), (right, left), None)]
    q_other = lax.dynamic_slice_in_dim(queries, (1 - parity) * (wide // 2), wide // 2, 1)
    q_got = lax.ppermute(q_other, "ctx", flip)
    got = lax.ppermute(other, "ctx", flip)
    far = [both((got, got), (right, left), None)]
    rows = wide // 2 // HD * 2 * tok
    turned, *state = pair_flash(
        functools.partial(pair_first_kernel, tok),
        tok, rows, (hit_count, queries, q_got, mine), (), False,
    )

    def absorb(step, part, pair, state):
        last = (step, part) == (levels - 1, 1)
        kernel = functools.partial(pair_step_kernel, n, tok, step, part, last)
        return pair_flash(kernel, tok, rows, (hit_count, turned, *pair), state, last)

    first = near_state = middle = state[0]
    for step in range(1, levels):
        if step == 2:
            near.append(both(near[-1], (right, left), None))
            far.append(both(far[-1], (right, left), first))
        elif step > 2:
            near.append(both(near[-1], (right, left), first))
            far.append(both(far[-1], (right, left), mid))
        state = absorb(step, 0, near[step - 1], state)
        near_state = state[0]
        if step == 1:
            state = absorb(0, 1, (got, got), state)
        middle = state[0]
        if step == 1:
            early, mid = near_state, middle
        state = absorb(step, 1, far[step - 1], state)
    attention = state

    held = [both((a, a), (right, left), None) for a in attention]
    buffer, token = (), None
    for step in range(1, half):
        arrived = held
        if step < half - 1:
            held = [both(pair, (right, left), token) for pair in arrived]
        else:
            held = [
                lax.ppermute(after(arrived[0][0], token), "ctx", right),
                lax.ppermute(after(arrived[1][1], token), "ctx", left),
            ]
        arrays = [arrived[k][side] for side in range(2) for k in range(2)]
        steps = (-step, step)
        if step == 1:
            arrays, steps = list(attention) + arrays, (0, -1, 1)
        buffer = (pair_project(n, steps, arrays, out_weight, buffer),)
        token = buffer[0]
    keep, *sends = pair_add(n, token)
    got = [lax.ppermute(send, "tp", swap) for send in sends]
    stay, send, other = pair_sort(after(keep, tuple(held)), got)
    got = lax.ppermute(send, "tp", over)
    keep, send = pair_far(n, held, out_weight, token)
    last_stay, last_send = pair_last(n, keep, lax.ppermute(send, "tp", swap), other)
    last_got = lax.ppermute(last_send, "tp", over)
    mine, give = pair_choose(n, stay, got, last_stay, last_got)
    return join(mine, lax.ppermute(give, "tp", swap))


def solution(mesh):
    n, n_tp = mesh.shape["ctx"], mesh.shape["tp"]
    placed = (
        P("ctx", "tp"),
        P(None, "ctx", "tp"),
        P(None, "ctx", None, "tp"),
        P(),
        P("ctx", None),
        P("tp", "ctx"),
    )

    def run(*arrays):
        slots_dev = arrays[1].shape[2] // HD
        paired = slots_dev == 2 and n_tp == 4 and n == 2 * n_tp
        return (pair_body if paired else body)(n, n_tp, *arrays)

    return jax.shard_map(
        run,
        mesh=mesh,
        in_specs=placed,
        out_specs=P("tp", "ctx"),
        check_vma=False,
    )
```

```python
import functools
import math

import jax
import jax.numpy as jnp
from jax import lax
from jax.experimental import pallas as pl
from jax.experimental.pallas import tpu as pltpu
from jax.sharding import PartitionSpec as P

HD = 128
HCAP = 3
neg_fill = -1e30
score_scale = 1.0 / math.sqrt(HD)
kernel_vmem = 16 * 1024 * 1024

vmem = pl.BlockSpec(memory_space=pltpu.VMEM)
smem = pl.BlockSpec(memory_space=pltpu.SMEM)
hbm = pl.BlockSpec(memory_space=pltpu.HBM)
params = pltpu.CompilerParams(vmem_limit_bytes=kernel_vmem)
light = pl.CostEstimate(flops=1000, bytes_accessed=1000, transcendentals=0)


def ring_order(n):
    return [2 * q if 2 * q < n else 2 * (n - 1 - q) + 1 for q in range(n)]


def owner_of(me, step, n):
    place = jnp.where(me % 2 == 0, me // 2, n - 1 - me // 2)
    place = lax.rem(place + step + n, n)
    return jnp.where(2 * place < n, 2 * place, 2 * (n - 1 - place) + 1)


def pick_kernel(blk, hit_slots, pool_ref, suffix_ref, near_ref, rest_ref, held, slots_ref, slots_sem, sems):
    outs = (near_ref, rest_ref)
    fetch = pltpu.make_async_copy(hit_slots, slots_ref, slots_sem)
    fetch.start()
    fetch.wait()
    copies = []
    for kv in range(2):
        for place in range(HCAP + 1):
            if place == 0:
                src = suffix_ref.at[kv]
            else:
                src = pool_ref.at[kv, slots_ref[0, place - 1]]
            if kv == 0:
                dst = outs[place // 2].at[0, pl.ds(place % 2 * blk, blk), :]
            else:
                dst = held.at[place]
            copies.append(pltpu.make_async_copy(src, dst, sems.at[kv, place]))
    for copy in copies:
        copy.start()
    for copy in copies:
        copy.wait()
    for place in range(HCAP + 1):
        for lane in range(0, held.shape[2], HD):
            at = slice(place % 2 * blk, (place % 2 + 1) * blk)
            outs[place // 2][1, at, lane : lane + HD] = held[place, :, lane : lane + HD].T


def pick(hit_slots, cache_pool, suffix_kv):
    blk, wide = cache_pool.shape[2:]
    return pl.pallas_call(
        functools.partial(pick_kernel, blk),
        out_shape=[jax.ShapeDtypeStruct((2, 2 * blk, wide), jnp.bfloat16)] * 2,
        in_specs=[hbm, hbm, hbm],
        out_specs=[vmem, vmem],
        scratch_shapes=[
            pltpu.VMEM((HCAP + 1, blk, wide), jnp.bfloat16),
            pltpu.SMEM(hit_slots.shape, jnp.int32),
            pltpu.SemaphoreType.DMA,
            pltpu.SemaphoreType.DMA((2, HCAP + 1)),
        ],
        compiler_params=pltpu.CompilerParams(vmem_limit_bytes=60 * 1024 * 1024),
        name="pick",
    )(hit_slots, cache_pool, suffix_kv)


def fold(op, array):
    parts = [array[r : r + 8] for r in range(0, array.shape[0], 8)]
    while len(parts) > 1:
        pairs = [op(a, b) for a, b in zip(parts[::2], parts[1::2])]
        parts = pairs + parts[len(parts) - len(parts) % 2 :]
    return parts[0]


def flash_kernel(n, tok, pieces, first, last, hit_ref, q_ref, *refs):
    count = len(pieces)
    kv_refs, refs = refs[:count], refs[count:]
    me = lax.axis_index("ctx")
    heads = (q_ref.shape[1] if first else q_ref.shape[1] // tok * HD) // HD
    keys, wide = kv_refs[0].shape[1:]
    blk = keys // 2
    slots_dev = wide // HD
    group = heads // slots_dev
    per = 2 if group % 2 == 0 else 1
    rows = per * tok
    biases = []
    for kind, step in pieces:
        owner = owner_of(me, step, n)
        if kind == 0:
            seen = [None if step == 0 else owner < me, None]
        else:
            seen = [hit_ref[owner] > 1, hit_ref[owner] > 2]
        biases.append([0.0 if s is None else jnp.where(s, 0.0, neg_fill) for s in seen])

    def place(j):
        head = j * per
        cols = [slice((head + h) * HD, (head + h + 1) * HD) for h in range(per)]
        slot = head // group
        return cols, slice(head * tok, head * tok + rows), slice(slot * HD, (slot + 1) * HD)

    def score(j):
        cols, at, lanes = place(j)
        if first:
            turned = jnp.concatenate([q_ref[:, c].T for c in cols], axis=1)
            refs[-4][:, at] = turned
        else:
            turned = q_ref[:, at]
        scores = []
        for (kind, step), ref, bias in zip(pieces, kv_refs, biases):
            raw = jnp.dot(ref[0, :, lanes], turned, preferred_element_type=jnp.float32)
            for b in range(2):
                part = raw[b * blk : (b + 1) * blk]
                if (kind, step, b) == (0, 0, 0):
                    key = lax.broadcasted_iota(jnp.int32, part.shape, 0)
                    token = lax.broadcasted_iota(jnp.int32, part.shape, 1) % tok
                    part = jnp.where(key <= token, part, neg_fill)
                scores.append((part, bias[b]))
        return scores

    def weigh(j, scores):
        _, at, _ = place(j)
        tops = [fold(jnp.maximum, part) + bias for part, bias in scores]
        top = jnp.max(functools.reduce(jnp.maximum, tops), axis=0, keepdims=True)
        total = fade = None
        if not first:
            m_in, l_in, _ = refs[:3]
            old_top = m_in[:, at]
            top = jnp.maximum(old_top, top)
            fade = jnp.exp((old_top - top) * score_scale)
            total = l_in[:, at] * fade
        if not last:
            refs[-3][:, at] = jnp.broadcast_to(top, (8, rows))
        offset = top[:1] * score_scale
        probs = []
        for part, bias in scores:
            weights = jnp.exp(part * score_scale - (offset - bias))
            add = fold(jnp.add, weights)
            total = add if total is None else total + add
            probs.append(weights.astype(jnp.bfloat16))
        if not last:
            refs[-2][:, at] = total
        return jnp.concatenate(probs, axis=0), fade, total

    def mix(j, probs, fade, total):
        cols, at, lanes = place(j)
        values = [ref[1, b * blk : (b + 1) * blk, lanes] for ref in kv_refs for b in range(2)]
        mixed = jnp.dot(
            jnp.concatenate(values, axis=1), probs, preferred_element_type=jnp.float32
        )
        if not first:
            mixed = mixed + refs[2][:, at] * fade[:1]
        if not last:
            refs[-1][:, at] = mixed
            return
        result = mixed * (1.0 / jnp.sum(total, axis=0, keepdims=True))
        half = tok // 2
        for h, c in enumerate(cols):
            head_out = result[:, h * tok : (h + 1) * tok].T.astype(jnp.bfloat16)
            for k, out in enumerate(refs[-2:]):
                out[:, c] = head_out[k * half : (k + 1) * half]

    blocks = heads // per
    ahead = min(2, blocks)
    scores = [score(j) for j in range(ahead)]
    for j in range(blocks):
        weighed = weigh(j, scores[j])
        scores[j] = None
        if j + ahead < blocks:
            scores.append(score(j + ahead))
        mix(j, *weighed)


def flash(n, tok, queries, hit_count, pieces, arrays, state, last):
    rows = queries.size // HD
    small = jax.ShapeDtypeStruct((8, rows), jnp.float32)
    if last:
        out_shape = [jax.ShapeDtypeStruct((tok // 2, rows // tok * HD), jnp.bfloat16)] * 2
        aliases = {}
    else:
        out_shape = [small, small, jax.ShapeDtypeStruct((HD, rows), jnp.float32)]
        aliases = {2 + len(arrays) + i: i for i in range(len(state))}
    if not state:
        out_shape = [jax.ShapeDtypeStruct((HD, rows), jnp.bfloat16)] + out_shape
    return pl.pallas_call(
        functools.partial(flash_kernel, n, tok, pieces, not state, last),
        out_shape=out_shape,
        in_specs=[smem] + [vmem] * (1 + len(arrays) + len(state)),
        out_specs=[vmem] * len(out_shape),
        input_output_aliases=aliases,
        compiler_params=params,
        cost_estimate=light,
        name="flash",
    )(hit_count, queries, *arrays, *state)


def project_kernel(count, *refs):
    shard_refs, (w_ref, keep_ref, send_ref) = refs[: 2 * count], refs[2 * count :]
    odd = lax.axis_index("tp") % 2
    rows = jnp.concatenate([ref[...] for ref in shard_refs], axis=0)
    half = rows.shape[0] // (2 * count)
    wide = w_ref.shape[1]
    width = min(256, wide)
    deep = w_ref.shape[0] // 2
    depths = (slice(0, deep), slice(deep, 2 * deep))
    for col in range(0, wide, width):
        at = slice(col, col + width)
        product = sum(
            jnp.dot(rows[:, k], w_ref[k, at], preferred_element_type=jnp.float32) for k in depths
        )
        product = product.astype(jnp.bfloat16)
        for i in range(count):
            low = product[2 * i * half : (2 * i + 1) * half]
            high = product[(2 * i + 1) * half : (2 * i + 2) * half]

            @pl.when(odd == 0)
            def _():
                keep_ref[i, :, at] = low
                send_ref[i, :, at] = high

            @pl.when(odd == 1)
            def _():
                keep_ref[i, :, at] = high
                send_ref[i, :, at] = low


def project(arrays, out_weight):
    half = arrays[0].shape[0]
    depth, wide = out_weight.shape
    count = len(arrays) // 2
    return pl.pallas_call(
        functools.partial(project_kernel, count),
        out_shape=[jax.ShapeDtypeStruct((count, half, wide), jnp.bfloat16)] * 2,
        in_specs=[vmem] * (len(arrays) + 1),
        out_specs=[vmem, vmem],
        compiler_params=params,
        cost_estimate=light,
        name="project",
    )(*arrays, out_weight)


def sides(n, n_tp, steps):
    me = lax.axis_index("ctx")
    my_tp = lax.axis_index("tp")
    share = n // n_tp
    found, near_count, away_count = [], jnp.int32(0), jnp.int32(0)
    for step in steps:
        owner = owner_of(me, step, n)
        away = lax.bitwise_xor(owner // share, my_tp) // 2 % 2
        found.append((owner, away, jnp.where(away == 1, away_count, near_count)))
        near_count = near_count + 1 - away
        away_count = away_count + away
    return found


def added(a, b):
    return a.astype(jnp.float32) + b.astype(jnp.float32)


def sort_kernel(n, n_tp, steps, *refs):
    *refs, stay_ref, send_ref, last_stay_ref, last_send_ref = refs
    count = len(refs) - len(steps)
    places = [(a, i) for a in refs[:count] for i in range(a.shape[0])]
    places = [(a, b, i) for (a, i), b in zip(places, refs[count:])]
    full = stay_ref.shape[0]
    for (a, b, i), (_, away, rank) in zip(places, sides(n, n_tp, steps)):
        total = added(a[i], b[0]).astype(jnp.bfloat16)
        for side, out, last in ((0, stay_ref, last_stay_ref), (1, send_ref, last_send_ref)):

            @pl.when((away == side) & (rank < full))
            def _():
                out[rank] = total

            @pl.when((away == side) & (rank == full))
            def _():
                last[0] = total


def sort(n, n_tp, steps, sums):
    keeps = [keep for keep, _ in sums]
    gots = [piece for _, pieces in sums for piece in pieces]
    half, wide = keeps[0].shape[1:]
    many = jax.ShapeDtypeStruct((n // 2 - 1, half, wide), jnp.bfloat16)
    one = jax.ShapeDtypeStruct((1, half, wide), jnp.bfloat16)
    return pl.pallas_call(
        functools.partial(sort_kernel, n, n_tp, steps),
        out_shape=[many, many, one, one],
        in_specs=[vmem] * (len(keeps) + len(gots)),
        out_specs=[vmem] * 4,
        compiler_params=params,
        cost_estimate=light,
        name="sort",
    )(*keeps, *gots)


def last_kernel(n, n_tp, keep_ref, got_ref, stay_in, send_in, stay_ref, send_ref):
    ((_, away, _),) = sides(n, n_tp, (n // 2,))
    total = added(keep_ref[...], got_ref[...]).astype(jnp.bfloat16)
    stay_ref[...] = jnp.where(away == 0, total, stay_in[...])
    send_ref[...] = jnp.where(away == 1, total, send_in[...])


def place_last(n, n_tp, keep, got, stay, send):
    return pl.pallas_call(
        functools.partial(last_kernel, n, n_tp),
        out_shape=[jax.ShapeDtypeStruct(keep.shape, jnp.bfloat16)] * 2,
        in_specs=[vmem] * 4,
        out_specs=[vmem] * 2,
        compiler_params=params,
        cost_estimate=light,
        name="last",
    )(keep, got, stay, send)


def choose_kernel(n, n_tp, steps, *refs):
    stay, got, last_stay, last_got, mine_ref, give_ref = refs
    my_tp = lax.axis_index("tp")
    share = n // n_tp
    found = sides(n, n_tp, steps)
    full = stay.shape[0]
    for r in range(full + 1):
        owner = jnp.int32(0)
        for candidate, away, rank in found:
            owner = jnp.where((away == 0) & (rank == r), candidate, owner)
        if r < full:
            total = added(stay[r], got[r])
        else:
            total = added(last_stay[0], last_got[0])
        for out, block in ((mine_ref, my_tp), (give_ref, lax.bitwise_xor(my_tp, 1))):

            @pl.when(owner // share == block)
            def _():
                out[owner % share] = total.astype(out.dtype)


def choose(n, n_tp, steps, arrays):
    half, wide = arrays[0].shape[1:]
    return pl.pallas_call(
        functools.partial(choose_kernel, n, n_tp, steps),
        out_shape=[jax.ShapeDtypeStruct((n // n_tp, half, wide), jnp.bfloat16)] * 2,
        in_specs=[vmem] * 4,
        out_specs=[vmem, vmem],
        compiler_params=params,
        name="choose",
    )(*arrays)


def join_kernel(mine_ref, got_ref, out_ref):
    odd = lax.axis_index("tp") % 2
    count, half, _ = mine_ref.shape
    for low in range(2):
        first, second = (mine_ref, got_ref) if low == 0 else (got_ref, mine_ref)

        @pl.when(odd == low)
        def _():
            for i in range(count):
                out_ref[2 * i * half : (2 * i + 1) * half] = first[i]
                out_ref[(2 * i + 1) * half : (2 * i + 2) * half] = second[i]


def join(mine, got):
    count, half, wide = mine.shape
    return pl.pallas_call(
        join_kernel,
        out_shape=jax.ShapeDtypeStruct((2 * count * half, wide), jnp.bfloat16),
        in_specs=[vmem, vmem],
        out_specs=vmem,
        compiler_params=params,
        name="join",
    )(mine, got)


def after(array, token):
    return lax.optimization_barrier((array, token))[0]


def body(n, n_tp, queries, suffix_kv, cache_pool, hit_count, hit_slots, out_weight):
    tok = queries.shape[0]
    half = n // 2
    order = ring_order(n)
    right = [(order[i], order[(i + 1) % n]) for i in range(n)]
    left = [(b, a) for a, b in right]

    def send_both(pair, k, token):
        from_left, from_right = pair
        if token is not None:
            from_left = after(from_left, token)
            from_right = after(from_right, token)
        return lax.ppermute(from_left, "ctx", right), lax.ppermute(from_right, "ctx", left)

    def ring(own, visit, token):
        held = [send_both((a, a), k, None) for k, a in enumerate(own)]
        for step in range(1, half):
            token = visit(step - 1, arrived if step > 1 else None, token)
            arrived = held
            if step < half - 1:
                held = [send_both(arrived[k], k, token) for k in range(2)]
            else:
                held = (
                    lax.ppermute(after(arrived[0][0], token), "ctx", right),
                    lax.ppermute(after(arrived[1][1], token), "ctx", left),
                )
        token = visit(half - 1, arrived, token)
        return held, token

    def absorb(step, arrived, state):
        if step == 0:
            return flash(n, tok, queries, hit_count, ((0, 0), (1, 0)), own, (), False)
        turned, state = state[0], state[1:]
        for kind in range(2):
            pieces = ((kind, -step), (kind, step))
            state = flash(n, tok, turned, hit_count, pieces, arrived[kind], state, False)
        return [turned] + list(state)

    own = pick(hit_slots, cache_pool, suffix_kv)
    far, state = ring(own, absorb, None)
    attention = flash(
        n, tok, state[0], hit_count, ((0, half), (1, half)), far, tuple(state[1:]), True
    )

    swap = [(t, t ^ 1) for t in range(n_tp)]
    sums = []

    def reduce(arrays):
        keep, send = project(arrays, out_weight)
        pieces = [send[i : i + 1] for i in range(send.shape[0])]
        sums.append((keep, [lax.ppermute(piece, "tp", swap) for piece in pieces]))
        return send

    def spread(step, arrived, token):
        if step == 0:
            return attention[0]
        (a_left, a_right), (b_left, b_right) = arrived
        arrays = (a_left, b_left, a_right, b_right)
        return reduce(tuple(attention) + arrays if step == 1 else arrays)

    def cross(stay, send):
        got = lax.ppermute(send, "tp", [(t, t ^ 2) for t in range(n_tp)])
        bit = 4
        while bit < n_tp:
            stay = added(stay, got).astype(jnp.bfloat16)
            got = lax.ppermute(stay, "tp", [(t, t ^ bit) for t in range(n_tp)])
            bit *= 2
        return stay, got

    far, _ = ring(attention, spread, None)
    steps = [0] + [s * d for d in range(1, half) for s in (-1, 1)] + [half]
    stay, send, last_stay, last_send = sort(n, n_tp, steps[:-1], sums)
    stay, got = cross(stay, send)
    reduce(far)
    keep, (piece,) = sums[-1]
    last_stay, last_send = place_last(n, n_tp, keep, piece, last_stay, last_send)
    last_stay, last_got = cross(last_stay, last_send)
    mine, give = choose(n, n_tp, steps, (stay, got, last_stay, last_got))
    return join(mine, lax.ppermute(give, "tp", swap))


def solution(mesh):
    n, n_tp = mesh.shape["ctx"], mesh.shape["tp"]
    placed = (
        P("ctx", "tp"),
        P(None, "ctx", "tp"),
        P(None, "ctx", None, "tp"),
        P(),
        P("ctx", None),
        P("tp", "ctx"),
    )
    return jax.shard_map(
        functools.partial(body, n, n_tp),
        mesh=mesh,
        in_specs=placed,
        out_specs=P("tp", "ctx"),
        check_vma=False,
    )
```

```python
import functools
import math

import jax
import jax.numpy as jnp
from jax import lax
from jax.experimental import pallas as pl
from jax.experimental.pallas import tpu as pltpu
from jax.sharding import PartitionSpec as P

HD = 128
HCAP = 3
neg_fill = -1e30
score_scale = 1.0 / math.sqrt(HD)
kernel_vmem = 16 * 1024 * 1024

vmem = pl.BlockSpec(memory_space=pltpu.VMEM)
smem = pl.BlockSpec(memory_space=pltpu.SMEM)
hbm = pl.BlockSpec(memory_space=pltpu.HBM)
params = pltpu.CompilerParams(vmem_limit_bytes=kernel_vmem)
light = pl.CostEstimate(flops=1000, bytes_accessed=1000, transcendentals=0)


def ring_order(n):
    return [2 * q if 2 * q < n else 2 * (n - 1 - q) + 1 for q in range(n)]


def owner_of(me, step, n):
    place = jnp.where(me % 2 == 0, me // 2, n - 1 - me // 2)
    place = lax.rem(place + step + n, n)
    return jnp.where(2 * place < n, 2 * place, 2 * (n - 1 - place) + 1)


def pick_kernel(blk, hit_slots, pool_ref, suffix_ref, near_ref, rest_ref, held, slots_ref, slots_sem, sems):
    outs = (near_ref, rest_ref)
    fetch = pltpu.make_async_copy(hit_slots, slots_ref, slots_sem)
    fetch.start()
    fetch.wait()
    copies = []
    for kv in range(2):
        for place in range(HCAP + 1):
            if place == 0:
                src = suffix_ref.at[kv]
            else:
                src = pool_ref.at[kv, slots_ref[0, place - 1]]
            if kv == 0:
                dst = outs[place // 2].at[0, pl.ds(place % 2 * blk, blk), :]
            else:
                dst = held.at[place]
            copies.append(pltpu.make_async_copy(src, dst, sems.at[kv, place]))
    for copy in copies:
        copy.start()
    for copy in copies:
        copy.wait()
    for place in range(HCAP + 1):
        for lane in range(0, held.shape[2], HD):
            at = slice(place % 2 * blk, (place % 2 + 1) * blk)
            outs[place // 2][1, at, lane : lane + HD] = held[place, :, lane : lane + HD].T


def pick(hit_slots, cache_pool, suffix_kv):
    blk, wide = cache_pool.shape[2:]
    return pl.pallas_call(
        functools.partial(pick_kernel, blk),
        out_shape=[jax.ShapeDtypeStruct((2, 2 * blk, wide), jnp.bfloat16)] * 2,
        in_specs=[hbm, hbm, hbm],
        out_specs=[vmem, vmem],
        scratch_shapes=[
            pltpu.VMEM((HCAP + 1, blk, wide), jnp.bfloat16),
            pltpu.SMEM(hit_slots.shape, jnp.int32),
            pltpu.SemaphoreType.DMA,
            pltpu.SemaphoreType.DMA((2, HCAP + 1)),
        ],
        compiler_params=pltpu.CompilerParams(vmem_limit_bytes=60 * 1024 * 1024),
        name="pick",
    )(hit_slots, cache_pool, suffix_kv)


def fold(op, array):
    parts = [array[r : r + 8] for r in range(0, array.shape[0], 8)]
    while len(parts) > 1:
        pairs = [op(a, b) for a, b in zip(parts[::2], parts[1::2])]
        parts = pairs + parts[len(parts) - len(parts) % 2 :]
    return parts[0]


def flash_kernel(n, tok, pieces, first, last, hit_ref, q_ref, *refs):
    count = len(pieces)
    kv_refs, refs = refs[:count], refs[count:]
    me = lax.axis_index("ctx")
    heads = (q_ref.shape[1] if first else q_ref.shape[1] // tok * HD) // HD
    keys, wide = kv_refs[0].shape[1:]
    blk = keys // 2
    slots_dev = wide // HD
    group = heads // slots_dev
    per = 2 if group % 2 == 0 else 1
    rows = per * tok
    biases = []
    for kind, step in pieces:
        owner = owner_of(me, step, n)
        if kind == 0:
            seen = [None if step == 0 else owner < me, None]
        else:
            seen = [hit_ref[owner] > 1, hit_ref[owner] > 2]
        biases.append([0.0 if s is None else jnp.where(s, 0.0, neg_fill) for s in seen])

    def place(j):
        head = j * per
        cols = [slice((head + h) * HD, (head + h + 1) * HD) for h in range(per)]
        slot = head // group
        return cols, slice(head * tok, head * tok + rows), slice(slot * HD, (slot + 1) * HD)

    def score(j):
        cols, at, lanes = place(j)
        if first:
            turned = jnp.concatenate([q_ref[:, c].T for c in cols], axis=1)
            refs[-4][:, at] = turned
        else:
            turned = q_ref[:, at]
        scores = []
        for (kind, step), ref, bias in zip(pieces, kv_refs, biases):
            raw = jnp.dot(ref[0, :, lanes], turned, preferred_element_type=jnp.float32)
            for b in range(2):
                part = raw[b * blk : (b + 1) * blk]
                if (kind, step, b) == (0, 0, 0):
                    key = lax.broadcasted_iota(jnp.int32, part.shape, 0)
                    token = lax.broadcasted_iota(jnp.int32, part.shape, 1) % tok
                    part = jnp.where(key <= token, part, neg_fill)
                scores.append((part, bias[b]))
        return scores

    def weigh(j, scores):
        _, at, _ = place(j)
        tops = [fold(jnp.maximum, part) + bias for part, bias in scores]
        top = jnp.max(functools.reduce(jnp.maximum, tops), axis=0, keepdims=True)
        total = fade = None
        if not first:
            m_in, l_in, _ = refs[:3]
            old_top = m_in[:, at]
            top = jnp.maximum(old_top, top)
            fade = jnp.exp((old_top - top) * score_scale)
            total = l_in[:, at] * fade
        if not last:
            refs[-3][:, at] = jnp.broadcast_to(top, (8, rows))
        offset = top[:1] * score_scale
        probs = []
        for part, bias in scores:
            weights = jnp.exp(part * score_scale - (offset - bias))
            add = fold(jnp.add, weights)
            total = add if total is None else total + add
            probs.append(weights.astype(jnp.bfloat16))
        if not last:
            refs[-2][:, at] = total
        return jnp.concatenate(probs, axis=0), fade, total

    def mix(j, probs, fade, total):
        cols, at, lanes = place(j)
        values = [ref[1, b * blk : (b + 1) * blk, lanes] for ref in kv_refs for b in range(2)]
        mixed = jnp.dot(
            jnp.concatenate(values, axis=1), probs, preferred_element_type=jnp.float32
        )
        if not first:
            mixed = mixed + refs[2][:, at] * fade[:1]
        if not last:
            refs[-1][:, at] = mixed
            return
        result = mixed * (1.0 / jnp.sum(total, axis=0, keepdims=True))
        half = tok // 2
        for h, c in enumerate(cols):
            head_out = result[:, h * tok : (h + 1) * tok].T.astype(jnp.bfloat16)
            for k, out in enumerate(refs[-2:]):
                out[:, c] = head_out[k * half : (k + 1) * half]

    blocks = heads // per
    ahead = min(2, blocks)
    scores = [score(j) for j in range(ahead)]
    for j in range(blocks):
        weighed = weigh(j, scores[j])
        scores[j] = None
        if j + ahead < blocks:
            scores.append(score(j + ahead))
        mix(j, *weighed)


def flash(n, tok, queries, hit_count, pieces, arrays, state, last):
    rows = queries.size // HD
    small = jax.ShapeDtypeStruct((8, rows), jnp.float32)
    if last:
        out_shape = [jax.ShapeDtypeStruct((tok // 2, rows // tok * HD), jnp.bfloat16)] * 2
        aliases = {}
    else:
        out_shape = [small, small, jax.ShapeDtypeStruct((HD, rows), jnp.float32)]
        aliases = {2 + len(arrays) + i: i for i in range(len(state))}
    if not state:
        out_shape = [jax.ShapeDtypeStruct((HD, rows), jnp.bfloat16)] + out_shape
    return pl.pallas_call(
        functools.partial(flash_kernel, n, tok, pieces, not state, last),
        out_shape=out_shape,
        in_specs=[smem] + [vmem] * (1 + len(arrays) + len(state)),
        out_specs=[vmem] * len(out_shape),
        input_output_aliases=aliases,
        compiler_params=params,
        cost_estimate=light,
        name="flash",
    )(hit_count, queries, *arrays, *state)


def project_kernel(count, *refs):
    shard_refs, (w_ref, keep_ref, send_ref) = refs[: 2 * count], refs[2 * count :]
    odd = lax.axis_index("tp") % 2
    rows = jnp.concatenate([ref[...] for ref in shard_refs], axis=0)
    half = rows.shape[0] // (2 * count)
    wide = w_ref.shape[1]
    width = min(256, wide)
    for col in range(0, wide, width):
        at = slice(col, col + width)
        product = jnp.dot(rows, w_ref[:, at], preferred_element_type=jnp.float32)
        product = product.astype(jnp.bfloat16)
        for i in range(count):
            low = product[2 * i * half : (2 * i + 1) * half]
            high = product[(2 * i + 1) * half : (2 * i + 2) * half]
            keep_ref[i, :, at] = jnp.where(odd == 0, low, high)
            send_ref[i, :, at] = jnp.where(odd == 0, high, low)


def project(arrays, out_weight):
    half = arrays[0].shape[0]
    depth, wide = out_weight.shape
    count = len(arrays) // 2
    return pl.pallas_call(
        functools.partial(project_kernel, count),
        out_shape=[jax.ShapeDtypeStruct((count, half, wide), jnp.bfloat16)] * 2,
        in_specs=[vmem] * (len(arrays) + 1),
        out_specs=[vmem, vmem],
        compiler_params=params,
        cost_estimate=light,
        name="project",
    )(*arrays, out_weight)


def sides(n, n_tp, steps):
    me = lax.axis_index("ctx")
    my_tp = lax.axis_index("tp")
    share = n // n_tp
    found, near_count, away_count = [], jnp.int32(0), jnp.int32(0)
    for step in steps:
        owner = owner_of(me, step, n)
        away = lax.bitwise_xor(owner // share, my_tp) // 2 % 2
        found.append((owner, away, jnp.where(away == 1, away_count, near_count)))
        near_count = near_count + 1 - away
        away_count = away_count + away
    return found


def added(a, b):
    return a.astype(jnp.float32) + b.astype(jnp.float32)


def sort_kernel(n, n_tp, steps, *refs):
    *refs, stay_ref, send_ref, last_stay_ref, last_send_ref = refs
    count = len(refs) // 2
    places = [(a, b, i) for a, b in zip(refs[:count], refs[count:]) for i in range(a.shape[0])]
    full = stay_ref.shape[0]
    for (a, b, i), (_, away, rank) in zip(places, sides(n, n_tp, steps)):
        total = added(a[i], b[i]).astype(jnp.bfloat16)
        for side, out, last in ((0, stay_ref, last_stay_ref), (1, send_ref, last_send_ref)):

            @pl.when((away == side) & (rank < full))
            def _():
                out[rank] = total

            @pl.when((away == side) & (rank == full))
            def _():
                last[0] = total


def sort(n, n_tp, steps, sums):
    keeps, gots = zip(*sums)
    half, wide = keeps[0].shape[1:]
    many = jax.ShapeDtypeStruct((n // 2 - 1, half, wide), jnp.bfloat16)
    one = jax.ShapeDtypeStruct((1, half, wide), jnp.bfloat16)
    return pl.pallas_call(
        functools.partial(sort_kernel, n, n_tp, steps),
        out_shape=[many, many, one, one],
        in_specs=[vmem] * (2 * len(sums)),
        out_specs=[vmem] * 4,
        compiler_params=params,
        cost_estimate=light,
        name="sort",
    )(*keeps, *gots)


def last_kernel(n, n_tp, keep_ref, got_ref, stay_in, send_in, stay_ref, send_ref):
    ((_, away, _),) = sides(n, n_tp, (n // 2,))
    total = added(keep_ref[...], got_ref[...]).astype(jnp.bfloat16)
    stay_ref[...] = jnp.where(away == 0, total, stay_in[...])
    send_ref[...] = jnp.where(away == 1, total, send_in[...])


def place_last(n, n_tp, keep, got, stay, send):
    return pl.pallas_call(
        functools.partial(last_kernel, n, n_tp),
        out_shape=[jax.ShapeDtypeStruct(keep.shape, jnp.bfloat16)] * 2,
        in_specs=[vmem] * 4,
        out_specs=[vmem] * 2,
        compiler_params=params,
        cost_estimate=light,
        name="last",
    )(keep, got, stay, send)


def choose_kernel(n, n_tp, steps, *refs):
    stay, got, last_stay, last_got, mine_ref, give_ref = refs
    my_tp = lax.axis_index("tp")
    share = n // n_tp
    found = sides(n, n_tp, steps)
    full = stay.shape[0]
    for r in range(full + 1):
        owner = jnp.int32(0)
        for candidate, away, rank in found:
            owner = jnp.where((away == 0) & (rank == r), candidate, owner)
        if r < full:
            total = added(stay[r], got[r])
        else:
            total = added(last_stay[0], last_got[0])
        for out, block in ((mine_ref, my_tp), (give_ref, lax.bitwise_xor(my_tp, 1))):

            @pl.when(owner // share == block)
            def _():
                out[owner % share] = total.astype(out.dtype)


def choose(n, n_tp, steps, arrays):
    half, wide = arrays[0].shape[1:]
    return pl.pallas_call(
        functools.partial(choose_kernel, n, n_tp, steps),
        out_shape=[jax.ShapeDtypeStruct((n // n_tp, half, wide), jnp.bfloat16)] * 2,
        in_specs=[vmem] * 4,
        out_specs=[vmem, vmem],
        compiler_params=params,
        name="choose",
    )(*arrays)


def join_kernel(mine_ref, got_ref, out_ref):
    odd = lax.axis_index("tp") % 2
    count, half, _ = mine_ref.shape
    for low in range(2):
        first, second = (mine_ref, got_ref) if low == 0 else (got_ref, mine_ref)

        @pl.when(odd == low)
        def _():
            for i in range(count):
                out_ref[2 * i * half : (2 * i + 1) * half] = first[i]
                out_ref[(2 * i + 1) * half : (2 * i + 2) * half] = second[i]


def join(mine, got):
    count, half, wide = mine.shape
    return pl.pallas_call(
        join_kernel,
        out_shape=jax.ShapeDtypeStruct((2 * count * half, wide), jnp.bfloat16),
        in_specs=[vmem, vmem],
        out_specs=vmem,
        compiler_params=params,
        name="join",
    )(mine, got)


def after(array, token):
    return lax.optimization_barrier((array, token))[0]


def body(n, n_tp, queries, suffix_kv, cache_pool, hit_count, hit_slots, out_weight):
    tok = queries.shape[0]
    half = n // 2
    order = ring_order(n)
    right = [(order[i], order[(i + 1) % n]) for i in range(n)]
    left = [(b, a) for a, b in right]

    def send_both(pair, k, token):
        from_left, from_right = pair
        if token is not None:
            from_left = after(from_left, token)
            from_right = after(from_right, token)
        return lax.ppermute(from_left, "ctx", right), lax.ppermute(from_right, "ctx", left)

    def ring(own, visit, token):
        held = [send_both((a, a), k, None) for k, a in enumerate(own)]
        for step in range(1, half):
            token = visit(step - 1, arrived if step > 1 else None, token)
            arrived = held
            if step < half - 1:
                held = [send_both(arrived[k], k, token) for k in range(2)]
            else:
                held = (
                    lax.ppermute(after(arrived[0][0], token), "ctx", right),
                    lax.ppermute(after(arrived[1][1], token), "ctx", left),
                )
        token = visit(half - 1, arrived, token)
        return held, token

    def absorb(step, arrived, state):
        if step == 0:
            return flash(n, tok, queries, hit_count, ((0, 0), (1, 0)), own, (), False)
        turned, state = state[0], state[1:]
        for kind in range(2):
            pieces = ((kind, -step), (kind, step))
            state = flash(n, tok, turned, hit_count, pieces, arrived[kind], state, False)
        return [turned] + list(state)

    own = pick(hit_slots, cache_pool, suffix_kv)
    far, state = ring(own, absorb, None)
    attention = flash(
        n, tok, state[0], hit_count, ((0, half), (1, half)), far, tuple(state[1:]), True
    )

    swap = [(t, t ^ 1) for t in range(n_tp)]
    sums = []

    def reduce(arrays):
        keep, send = project(arrays, out_weight)
        sums.append((keep, lax.ppermute(send, "tp", swap)))
        return send

    def spread(step, arrived, token):
        if step == 0:
            return attention[0]
        (a_left, a_right), (b_left, b_right) = arrived
        arrays = (a_left, b_left, a_right, b_right)
        return reduce(tuple(attention) + arrays if step == 1 else arrays)

    def cross(stay, send):
        got = lax.ppermute(send, "tp", [(t, t ^ 2) for t in range(n_tp)])
        bit = 4
        while bit < n_tp:
            stay = added(stay, got).astype(jnp.bfloat16)
            got = lax.ppermute(stay, "tp", [(t, t ^ bit) for t in range(n_tp)])
            bit *= 2
        return stay, got

    far, _ = ring(attention, spread, None)
    steps = [0] + [s * d for d in range(1, half) for s in (-1, 1)] + [half]
    sums[0] = (after(sums[0][0], far), sums[0][1])
    stay, send, last_stay, last_send = sort(n, n_tp, steps[:-1], sums)
    stay, got = cross(stay, send)
    reduce(far)
    last_stay, last_send = place_last(n, n_tp, *sums[-1], last_stay, last_send)
    last_stay, last_got = cross(last_stay, last_send)
    mine, give = choose(n, n_tp, steps, (stay, got, last_stay, last_got))
    return join(mine, lax.ppermute(give, "tp", swap))


def solution(mesh):
    n, n_tp = mesh.shape["ctx"], mesh.shape["tp"]
    placed = (
        P("ctx", "tp"),
        P(None, "ctx", "tp"),
        P(None, "ctx", None, "tp"),
        P(),
        P("ctx", None),
        P("tp", "ctx"),
    )
    return jax.shard_map(
        functools.partial(body, n, n_tp),
        mesh=mesh,
        in_specs=placed,
        out_specs=P("tp", "ctx"),
        check_vma=False,
    )
```

```python
import functools
import math

import jax
import jax.numpy as jnp
from jax import lax
from jax.experimental import pallas as pl
from jax.experimental.pallas import tpu as pltpu
from jax.sharding import PartitionSpec as P

HD = 128
HCAP = 3
neg_fill = -1e30
score_scale = 1.0 / math.sqrt(HD)
kernel_vmem = 16 * 1024 * 1024

vmem = pl.BlockSpec(memory_space=pltpu.VMEM)
smem = pl.BlockSpec(memory_space=pltpu.SMEM)
hbm = pl.BlockSpec(memory_space=pltpu.HBM)
params = pltpu.CompilerParams(vmem_limit_bytes=kernel_vmem)
light = pl.CostEstimate(flops=1000, bytes_accessed=1000, transcendentals=0)


def ring_order(n):
    return [2 * q if 2 * q < n else 2 * (n - 1 - q) + 1 for q in range(n)]


def owner_of(me, step, n):
    place = jnp.where(me % 2 == 0, me // 2, n - 1 - me // 2)
    place = lax.rem(place + step + n, n)
    return jnp.where(2 * place < n, 2 * place, 2 * (n - 1 - place) + 1)


def pick_kernel(blk, hit_slots, pool_ref, suffix_ref, near_ref, rest_ref, held, slots_ref, slots_sem, sems):
    outs = (near_ref, rest_ref)
    fetch = pltpu.make_async_copy(hit_slots, slots_ref, slots_sem)
    fetch.start()
    fetch.wait()
    copies = []
    for kv in range(2):
        for place in range(HCAP + 1):
            if place == 0:
                src = suffix_ref.at[kv]
            else:
                src = pool_ref.at[kv, slots_ref[0, place - 1]]
            if kv == 0:
                dst = outs[place // 2].at[0, pl.ds(place % 2 * blk, blk), :]
            else:
                dst = held.at[place]
            copies.append(pltpu.make_async_copy(src, dst, sems.at[kv, place]))
    for copy in copies:
        copy.start()
    for copy in copies:
        copy.wait()
    for place in range(HCAP + 1):
        for lane in range(0, held.shape[2], HD):
            at = slice(place % 2 * blk, (place % 2 + 1) * blk)
            outs[place // 2][1, at, lane : lane + HD] = held[place, :, lane : lane + HD].T


def pick(hit_slots, cache_pool, suffix_kv):
    blk, wide = cache_pool.shape[2:]
    return pl.pallas_call(
        functools.partial(pick_kernel, blk),
        out_shape=[jax.ShapeDtypeStruct((2, 2 * blk, wide), jnp.bfloat16)] * 2,
        in_specs=[hbm, hbm, hbm],
        out_specs=[vmem, vmem],
        scratch_shapes=[
            pltpu.VMEM((HCAP + 1, blk, wide), jnp.bfloat16),
            pltpu.SMEM(hit_slots.shape, jnp.int32),
            pltpu.SemaphoreType.DMA,
            pltpu.SemaphoreType.DMA((2, HCAP + 1)),
        ],
        compiler_params=pltpu.CompilerParams(vmem_limit_bytes=60 * 1024 * 1024),
        name="pick",
    )(hit_slots, cache_pool, suffix_kv)


def fold(op, array):
    parts = [array[r : r + 8] for r in range(0, array.shape[0], 8)]
    while len(parts) > 1:
        pairs = [op(a, b) for a, b in zip(parts[::2], parts[1::2])]
        parts = pairs + parts[len(parts) - len(parts) % 2 :]
    return parts[0]


def flash_kernel(n, tok, pieces, first, last, hit_ref, q_ref, *refs):
    count = len(pieces)
    kv_refs, refs = refs[:count], refs[count:]
    me = lax.axis_index("ctx")
    heads = (q_ref.shape[1] if first else q_ref.shape[1] // tok * HD) // HD
    keys, wide = kv_refs[0].shape[1:]
    blk = keys // 2
    slots_dev = wide // HD
    group = heads // slots_dev
    per = 2 if group % 2 == 0 else 1
    rows = per * tok
    biases = []
    for kind, step in pieces:
        owner = owner_of(me, step, n)
        if kind == 0:
            seen = [None if step == 0 else owner < me, None]
        else:
            seen = [hit_ref[owner] > 1, hit_ref[owner] > 2]
        biases.append([0.0 if s is None else jnp.where(s, 0.0, neg_fill) for s in seen])

    def place(j):
        head = j * per
        cols = [slice((head + h) * HD, (head + h + 1) * HD) for h in range(per)]
        slot = head // group
        return cols, slice(head * tok, head * tok + rows), slice(slot * HD, (slot + 1) * HD)

    def score(j):
        cols, at, lanes = place(j)
        if first:
            turned = jnp.concatenate([q_ref[:, c].T for c in cols], axis=1)
            refs[-4][:, at] = turned
        else:
            turned = q_ref[:, at]
        scores = []
        for (kind, step), ref, bias in zip(pieces, kv_refs, biases):
            raw = jnp.dot(ref[0, :, lanes], turned, preferred_element_type=jnp.float32)
            for b in range(2):
                part = raw[b * blk : (b + 1) * blk]
                if (kind, step, b) == (0, 0, 0):
                    key = lax.broadcasted_iota(jnp.int32, part.shape, 0)
                    token = lax.broadcasted_iota(jnp.int32, part.shape, 1) % tok
                    part = jnp.where(key <= token, part, neg_fill)
                scores.append((part, bias[b]))
        return scores

    def weigh(j, scores):
        _, at, _ = place(j)
        tops = [fold(jnp.maximum, part) + bias for part, bias in scores]
        top = jnp.max(functools.reduce(jnp.maximum, tops), axis=0, keepdims=True)
        total = fade = None
        if not first:
            m_in, l_in, _ = refs[:3]
            old_top = m_in[:, at]
            top = jnp.maximum(old_top, top)
            fade = jnp.exp((old_top - top) * score_scale)
            total = l_in[:, at] * fade
        if not last:
            refs[-3][:, at] = jnp.broadcast_to(top, (8, rows))
        offset = top[:1] * score_scale
        probs = []
        for part, bias in scores:
            weights = jnp.exp(part * score_scale - (offset - bias))
            add = fold(jnp.add, weights)
            total = add if total is None else total + add
            probs.append(weights.astype(jnp.bfloat16))
        if not last:
            refs[-2][:, at] = total
        return jnp.concatenate(probs, axis=0), fade, total

    def mix(j, probs, fade, total):
        cols, at, lanes = place(j)
        values = [ref[1, b * blk : (b + 1) * blk, lanes] for ref in kv_refs for b in range(2)]
        mixed = jnp.dot(
            jnp.concatenate(values, axis=1), probs, preferred_element_type=jnp.float32
        )
        if not first:
            mixed = mixed + refs[2][:, at] * fade[:1]
        if not last:
            refs[-1][:, at] = mixed
            return
        result = mixed * (1.0 / jnp.sum(total, axis=0, keepdims=True))
        half = tok // 2
        for h, c in enumerate(cols):
            head_out = result[:, h * tok : (h + 1) * tok].T.astype(jnp.bfloat16)
            for k, out in enumerate(refs[-2:]):
                out[:, c] = head_out[k * half : (k + 1) * half]

    blocks = heads // per
    ahead = min(2, blocks)
    scores = [score(j) for j in range(ahead)]
    for j in range(blocks):
        weighed = weigh(j, scores[j])
        scores[j] = None
        if j + ahead < blocks:
            scores.append(score(j + ahead))
        mix(j, *weighed)


def flash(n, tok, queries, hit_count, pieces, arrays, state, last):
    rows = queries.size // HD
    small = jax.ShapeDtypeStruct((8, rows), jnp.float32)
    if last:
        out_shape = [jax.ShapeDtypeStruct((tok // 2, rows // tok * HD), jnp.bfloat16)] * 2
        aliases = {}
    else:
        out_shape = [small, small, jax.ShapeDtypeStruct((HD, rows), jnp.float32)]
        aliases = {2 + len(arrays) + i: i for i in range(len(state))}
    if not state:
        out_shape = [jax.ShapeDtypeStruct((HD, rows), jnp.bfloat16)] + out_shape
    return pl.pallas_call(
        functools.partial(flash_kernel, n, tok, pieces, not state, last),
        out_shape=out_shape,
        in_specs=[smem] + [vmem] * (1 + len(arrays) + len(state)),
        out_specs=[vmem] * len(out_shape),
        input_output_aliases=aliases,
        compiler_params=params,
        cost_estimate=light,
        name="flash",
    )(hit_count, queries, *arrays, *state)


def project_kernel(count, *refs):
    shard_refs, (w_ref, keep_ref, send_ref) = refs[: 2 * count], refs[2 * count :]
    odd = lax.axis_index("tp") % 2
    rows = jnp.concatenate([ref[...] for ref in shard_refs], axis=0)
    half = rows.shape[0] // (2 * count)
    wide = w_ref.shape[1]
    width = min(256, wide)
    for col in range(0, wide, width):
        at = slice(col, col + width)
        product = jnp.dot(rows, w_ref[:, at], preferred_element_type=jnp.float32)
        product = product.astype(jnp.bfloat16)
        for i in range(count):
            low = product[2 * i * half : (2 * i + 1) * half]
            high = product[(2 * i + 1) * half : (2 * i + 2) * half]
            keep_ref[i, :, at] = jnp.where(odd == 0, low, high)
            send_ref[i, :, at] = jnp.where(odd == 0, high, low)


def project(arrays, out_weight):
    half = arrays[0].shape[0]
    depth, wide = out_weight.shape
    count = len(arrays) // 2
    return pl.pallas_call(
        functools.partial(project_kernel, count),
        out_shape=[jax.ShapeDtypeStruct((count, half, wide), jnp.bfloat16)] * 2,
        in_specs=[vmem] * (len(arrays) + 1),
        out_specs=[vmem, vmem],
        compiler_params=params,
        cost_estimate=light,
        name="project",
    )(*arrays, out_weight)


def sides(n, n_tp, steps):
    me = lax.axis_index("ctx")
    my_tp = lax.axis_index("tp")
    share = n // n_tp
    found, near_count, away_count = [], jnp.int32(0), jnp.int32(0)
    for step in steps:
        owner = owner_of(me, step, n)
        away = lax.bitwise_xor(owner // share, my_tp) // 2 % 2
        found.append((owner, away, jnp.where(away == 1, away_count, near_count)))
        near_count = near_count + 1 - away
        away_count = away_count + away
    return found


def added(a, b):
    return a.astype(jnp.float32) + b.astype(jnp.float32)


def sort_kernel(n, n_tp, steps, side, *refs):
    *refs, out, last = refs
    count = len(refs) // 2
    places = [(a, b, i) for a, b in zip(refs[:count], refs[count:]) for i in range(a.shape[0])]
    full = out.shape[0]
    for (a, b, i), (_, away, rank) in zip(places, sides(n, n_tp, steps)):
        total = added(a[i], b[i]).astype(jnp.bfloat16)

        @pl.when((away == side) & (rank < full))
        def _():
            out[rank] = total

        @pl.when((away == side) & (rank == full))
        def _():
            last[0] = total


def sort(n, n_tp, steps, side, sums):
    keeps, gots = zip(*sums)
    half, wide = keeps[0].shape[1:]
    many = jax.ShapeDtypeStruct((n // 2 - 1, half, wide), jnp.bfloat16)
    one = jax.ShapeDtypeStruct((1, half, wide), jnp.bfloat16)
    return pl.pallas_call(
        functools.partial(sort_kernel, n, n_tp, steps, side),
        out_shape=[many, one],
        in_specs=[vmem] * (2 * len(sums)),
        out_specs=[vmem] * 2,
        compiler_params=params,
        cost_estimate=light,
        name="sort",
    )(*keeps, *gots)


def last_kernel(n, n_tp, keep_ref, got_ref, stay_in, send_in, stay_ref, send_ref):
    ((_, away, _),) = sides(n, n_tp, (n // 2,))
    total = added(keep_ref[...], got_ref[...]).astype(jnp.bfloat16)
    stay_ref[...] = jnp.where(away == 0, total, stay_in[...])
    send_ref[...] = jnp.where(away == 1, total, send_in[...])


def place_last(n, n_tp, keep, got, stay, send):
    return pl.pallas_call(
        functools.partial(last_kernel, n, n_tp),
        out_shape=[jax.ShapeDtypeStruct(keep.shape, jnp.bfloat16)] * 2,
        in_specs=[vmem] * 4,
        out_specs=[vmem] * 2,
        compiler_params=params,
        cost_estimate=light,
        name="last",
    )(keep, got, stay, send)


def choose_kernel(n, n_tp, steps, *refs):
    stay, got, last_stay, last_got, mine_ref, give_ref = refs
    my_tp = lax.axis_index("tp")
    share = n // n_tp
    found = sides(n, n_tp, steps)
    full = stay.shape[0]
    for r in range(full + 1):
        owner = jnp.int32(0)
        for candidate, away, rank in found:
            owner = jnp.where((away == 0) & (rank == r), candidate, owner)
        if r < full:
            total = added(stay[r], got[r])
        else:
            total = added(last_stay[0], last_got[0])
        for out, block in ((mine_ref, my_tp), (give_ref, lax.bitwise_xor(my_tp, 1))):

            @pl.when(owner // share == block)
            def _():
                out[owner % share] = total.astype(out.dtype)


def choose(n, n_tp, steps, arrays):
    half, wide = arrays[0].shape[1:]
    return pl.pallas_call(
        functools.partial(choose_kernel, n, n_tp, steps),
        out_shape=[jax.ShapeDtypeStruct((n // n_tp, half, wide), jnp.bfloat16)] * 2,
        in_specs=[vmem] * 4,
        out_specs=[vmem, vmem],
        compiler_params=params,
        name="choose",
    )(*arrays)


def join_kernel(mine_ref, got_ref, out_ref, sems):
    odd = lax.axis_index("tp") % 2
    count, half, _ = mine_ref.shape
    copies = []
    for k, (ref, place) in enumerate(((mine_ref, odd), (got_ref, 1 - odd))):
        for i in range(count):
            at = pl.ds(pl.multiple_of((2 * i + place) * half, half), half)
            copies.append(pltpu.make_async_copy(ref.at[i], out_ref.at[at, :], sems.at[k, i]))
    for copy in copies:
        copy.start()
    for copy in copies:
        copy.wait()


def join(mine, got):
    count, half, wide = mine.shape
    return pl.pallas_call(
        join_kernel,
        out_shape=jax.ShapeDtypeStruct((2 * count * half, wide), jnp.bfloat16),
        in_specs=[vmem, vmem],
        out_specs=hbm,
        scratch_shapes=[pltpu.SemaphoreType.DMA((2, count))],
        compiler_params=params,
        name="join",
    )(mine, got)


def after(array, token):
    return lax.optimization_barrier((array, token))[0]


def body(n, n_tp, queries, suffix_kv, cache_pool, hit_count, hit_slots, out_weight):
    tok = queries.shape[0]
    half = n // 2
    order = ring_order(n)
    right = [(order[i], order[(i + 1) % n]) for i in range(n)]
    left = [(b, a) for a, b in right]

    def send_both(pair, k, token):
        from_left, from_right = pair
        if token is not None:
            from_left = after(from_left, token)
            from_right = after(from_right, token)
        return lax.ppermute(from_left, "ctx", right), lax.ppermute(from_right, "ctx", left)

    def ring(own, visit, token):
        held = [send_both((a, a), k, None) for k, a in enumerate(own)]
        for step in range(1, half):
            token = visit(step - 1, arrived if step > 1 else None, token)
            arrived = held
            if step < half - 1:
                held = [send_both(arrived[k], k, token) for k in range(2)]
            else:
                held = (
                    lax.ppermute(after(arrived[0][0], token), "ctx", right),
                    lax.ppermute(after(arrived[1][1], token), "ctx", left),
                )
        token = visit(half - 1, arrived, token)
        return held, token

    def absorb(step, arrived, state):
        if step == 0:
            return flash(n, tok, queries, hit_count, ((0, 0), (1, 0)), own, (), False)
        turned, state = state[0], state[1:]
        for kind in range(2):
            pieces = ((kind, -step), (kind, step))
            state = flash(n, tok, turned, hit_count, pieces, arrived[kind], state, False)
        return [turned] + list(state)

    own = pick(hit_slots, cache_pool, suffix_kv)
    far, state = ring(own, absorb, None)
    attention = flash(
        n, tok, state[0], hit_count, ((0, half), (1, half)), far, tuple(state[1:]), True
    )

    swap = [(t, t ^ 1) for t in range(n_tp)]
    sums = []

    def reduce(arrays):
        keep, send = project(arrays, out_weight)
        sums.append((keep, lax.ppermute(send, "tp", swap)))
        return send

    def spread(step, arrived, token):
        if step == 0:
            return attention[0]
        (a_left, a_right), (b_left, b_right) = arrived
        arrays = (a_left, b_left, a_right, b_right)
        return reduce(tuple(attention) + arrays if step == 1 else arrays)

    def cross(stay, send):
        got = lax.ppermute(send, "tp", [(t, t ^ 2) for t in range(n_tp)])
        bit = 4
        while bit < n_tp:
            stay = added(stay, got).astype(jnp.bfloat16)
            got = lax.ppermute(stay, "tp", [(t, t ^ bit) for t in range(n_tp)])
            bit *= 2
        return stay, got

    far, _ = ring(attention, spread, None)
    steps = [0] + [s * d for d in range(1, half) for s in (-1, 1)] + [half]
    sums[0] = (after(sums[0][0], far), sums[0][1])
    send, last_send = sort(n, n_tp, steps[:-1], 1, sums)
    kept = [(after(sums[0][0], send), sums[0][1])] + sums[1:]
    stay, last_stay = sort(n, n_tp, steps[:-1], 0, kept)
    stay, got = cross(stay, send)
    reduce(far)
    last_stay, last_send = place_last(n, n_tp, *sums[-1], last_stay, last_send)
    last_stay, last_got = cross(last_stay, last_send)
    mine, give = choose(n, n_tp, steps, (stay, got, last_stay, last_got))
    return join(mine, lax.ppermute(give, "tp", swap))


def solution(mesh):
    n, n_tp = mesh.shape["ctx"], mesh.shape["tp"]
    placed = (
        P("ctx", "tp"),
        P(None, "ctx", "tp"),
        P(None, "ctx", None, "tp"),
        P(),
        P("ctx", None),
        P("tp", "ctx"),
    )
    return jax.shard_map(
        functools.partial(body, n, n_tp),
        mesh=mesh,
        in_specs=placed,
        out_specs=P("tp", "ctx"),
        check_vma=False,
    )
```

```python
import functools
import math

import jax
import jax.numpy as jnp
from jax import lax
from jax.experimental import pallas as pl
from jax.experimental.pallas import tpu as pltpu
from jax.sharding import PartitionSpec as P

HD = 128
HCAP = 3
neg_fill = -1e30
score_scale = 1.0 / math.sqrt(HD)
kernel_vmem = 16 * 1024 * 1024

vmem = pl.BlockSpec(memory_space=pltpu.VMEM)
smem = pl.BlockSpec(memory_space=pltpu.SMEM)
hbm = pl.BlockSpec(memory_space=pltpu.HBM)
params = pltpu.CompilerParams(vmem_limit_bytes=kernel_vmem)
light = pl.CostEstimate(flops=1000, bytes_accessed=1000, transcendentals=0)


def ring_order(n):
    return [2 * q if 2 * q < n else 2 * (n - 1 - q) + 1 for q in range(n)]


def owner_of(me, step, n):
    place = jnp.where(me % 2 == 0, me // 2, n - 1 - me // 2)
    place = lax.rem(place + step + n, n)
    return jnp.where(2 * place < n, 2 * place, 2 * (n - 1 - place) + 1)


def pick_kernel(blk, hit_slots, pool_ref, suffix_ref, near_ref, rest_ref, held, slots_ref, slots_sem, sems):
    outs = (near_ref, rest_ref)
    fetch = pltpu.make_async_copy(hit_slots, slots_ref, slots_sem)
    fetch.start()
    fetch.wait()
    copies = []
    for kv in range(2):
        for place in range(HCAP + 1):
            if place == 0:
                src = suffix_ref.at[kv]
            else:
                src = pool_ref.at[kv, slots_ref[0, place - 1]]
            if kv == 0:
                dst = outs[place // 2].at[0, pl.ds(place % 2 * blk, blk), :]
            else:
                dst = held.at[place]
            copies.append(pltpu.make_async_copy(src, dst, sems.at[kv, place]))
    for copy in copies:
        copy.start()
    for copy in copies:
        copy.wait()
    for place in range(HCAP + 1):
        for lane in range(0, held.shape[2], HD):
            at = slice(place % 2 * blk, (place % 2 + 1) * blk)
            outs[place // 2][1, at, lane : lane + HD] = held[place, :, lane : lane + HD].T


def pick(hit_slots, cache_pool, suffix_kv):
    blk, wide = cache_pool.shape[2:]
    return pl.pallas_call(
        functools.partial(pick_kernel, blk),
        out_shape=[jax.ShapeDtypeStruct((2, 2 * blk, wide), jnp.bfloat16)] * 2,
        in_specs=[hbm, hbm, hbm],
        out_specs=[vmem, vmem],
        scratch_shapes=[
            pltpu.VMEM((HCAP + 1, blk, wide), jnp.bfloat16),
            pltpu.SMEM(hit_slots.shape, jnp.int32),
            pltpu.SemaphoreType.DMA,
            pltpu.SemaphoreType.DMA((2, HCAP + 1)),
        ],
        compiler_params=pltpu.CompilerParams(vmem_limit_bytes=60 * 1024 * 1024),
        name="pick",
    )(hit_slots, cache_pool, suffix_kv)


def fold(op, array):
    parts = [array[r : r + 8] for r in range(0, array.shape[0], 8)]
    while len(parts) > 1:
        pairs = [op(a, b) for a, b in zip(parts[::2], parts[1::2])]
        parts = pairs + parts[len(parts) - len(parts) % 2 :]
    return parts[0]


def flash_kernel(n, tok, pieces, first, last, hit_ref, q_ref, *refs):
    count = len(pieces)
    kv_refs, refs = refs[:count], refs[count:]
    me = lax.axis_index("ctx")
    heads = (q_ref.shape[1] if first else q_ref.shape[1] // tok * HD) // HD
    keys, wide = kv_refs[0].shape[1:]
    blk = keys // 2
    slots_dev = wide // HD
    group = heads // slots_dev
    per = 2 if group % 2 == 0 else 1
    rows = per * tok
    biases = []
    for kind, step in pieces:
        owner = owner_of(me, step, n)
        if kind == 0:
            seen = [None if step == 0 else owner < me, None]
        else:
            seen = [hit_ref[owner] > 1, hit_ref[owner] > 2]
        biases.append([0.0 if s is None else jnp.where(s, 0.0, neg_fill) for s in seen])

    def place(j):
        head = j * per
        cols = [slice((head + h) * HD, (head + h + 1) * HD) for h in range(per)]
        slot = head // group
        return cols, slice(head * tok, head * tok + rows), slice(slot * HD, (slot + 1) * HD)

    def score(j):
        cols, at, lanes = place(j)
        if first:
            turned = jnp.concatenate([q_ref[:, c].T for c in cols], axis=1)
            refs[-4][:, at] = turned
        else:
            turned = q_ref[:, at]
        scores = []
        for (kind, step), ref, bias in zip(pieces, kv_refs, biases):
            raw = jnp.dot(ref[0, :, lanes], turned, preferred_element_type=jnp.float32)
            for b in range(2):
                part = raw[b * blk : (b + 1) * blk]
                if (kind, step, b) == (0, 0, 0):
                    key = lax.broadcasted_iota(jnp.int32, part.shape, 0)
                    token = lax.broadcasted_iota(jnp.int32, part.shape, 1) % tok
                    part = jnp.where(key <= token, part, neg_fill)
                scores.append((part, bias[b]))
        return scores

    def weigh(j, scores):
        _, at, _ = place(j)
        tops = [fold(jnp.maximum, part) + bias for part, bias in scores]
        top = jnp.max(functools.reduce(jnp.maximum, tops), axis=0, keepdims=True)
        total = fade = None
        if not first:
            m_in, l_in, _ = refs[:3]
            old_top = m_in[:, at]
            top = jnp.maximum(old_top, top)
            fade = jnp.exp((old_top - top) * score_scale)
            total = l_in[:, at] * fade
        if not last:
            refs[-3][:, at] = jnp.broadcast_to(top, (8, rows))
        offset = top[:1] * score_scale
        probs = []
        for part, bias in scores:
            weights = jnp.exp(part * score_scale - (offset - bias))
            add = fold(jnp.add, weights)
            total = add if total is None else total + add
            probs.append(weights.astype(jnp.bfloat16))
        if not last:
            refs[-2][:, at] = total
        return jnp.concatenate(probs, axis=0), fade, total

    def mix(j, probs, fade, total):
        cols, at, lanes = place(j)
        values = [ref[1, b * blk : (b + 1) * blk, lanes] for ref in kv_refs for b in range(2)]
        mixed = jnp.dot(
            jnp.concatenate(values, axis=1), probs, preferred_element_type=jnp.float32
        )
        if not first:
            mixed = mixed + refs[2][:, at] * fade[:1]
        if not last:
            refs[-1][:, at] = mixed
            return
        result = mixed * (1.0 / jnp.sum(total, axis=0, keepdims=True))
        half = tok // 2
        for h, c in enumerate(cols):
            head_out = result[:, h * tok : (h + 1) * tok].T.astype(jnp.bfloat16)
            for k, out in enumerate(refs[-2:]):
                out[:, c] = head_out[k * half : (k + 1) * half]

    blocks = heads // per
    ahead = min(2, blocks)
    scores = [score(j) for j in range(ahead)]
    for j in range(blocks):
        weighed = weigh(j, scores[j])
        scores[j] = None
        if j + ahead < blocks:
            scores.append(score(j + ahead))
        mix(j, *weighed)


def flash(n, tok, queries, hit_count, pieces, arrays, state, last):
    rows = queries.size // HD
    small = jax.ShapeDtypeStruct((8, rows), jnp.float32)
    if last:
        out_shape = [jax.ShapeDtypeStruct((tok // 2, rows // tok * HD), jnp.bfloat16)] * 2
        aliases = {}
    else:
        out_shape = [small, small, jax.ShapeDtypeStruct((HD, rows), jnp.float32)]
        aliases = {2 + len(arrays) + i: i for i in range(len(state))}
    if not state:
        out_shape = [jax.ShapeDtypeStruct((HD, rows), jnp.bfloat16)] + out_shape
    return pl.pallas_call(
        functools.partial(flash_kernel, n, tok, pieces, not state, last),
        out_shape=out_shape,
        in_specs=[smem] + [vmem] * (1 + len(arrays) + len(state)),
        out_specs=[vmem] * len(out_shape),
        input_output_aliases=aliases,
        compiler_params=params,
        cost_estimate=light,
        name="flash",
    )(hit_count, queries, *arrays, *state)


def project_kernel(count, *refs):
    shard_refs, (w_ref, keep_ref, send_ref) = refs[: 2 * count], refs[2 * count :]
    odd = lax.axis_index("tp") % 2
    rows = jnp.concatenate([ref[...] for ref in shard_refs], axis=0)
    half = rows.shape[0] // (2 * count)
    wide = w_ref.shape[1]
    width = min(256, wide)
    for col in range(0, wide, width):
        at = slice(col, col + width)
        product = jnp.dot(rows, w_ref[:, at], preferred_element_type=jnp.float32)
        product = product.astype(jnp.bfloat16)
        for i in range(count):
            low = product[2 * i * half : (2 * i + 1) * half]
            high = product[(2 * i + 1) * half : (2 * i + 2) * half]
            keep_ref[i, :, at] = jnp.where(odd == 0, low, high)
            send_ref[i, :, at] = jnp.where(odd == 0, high, low)


def project(arrays, out_weight):
    half = arrays[0].shape[0]
    depth, wide = out_weight.shape
    count = len(arrays) // 2
    return pl.pallas_call(
        functools.partial(project_kernel, count),
        out_shape=[jax.ShapeDtypeStruct((count, half, wide), jnp.bfloat16)] * 2,
        in_specs=[vmem] * (len(arrays) + 1),
        out_specs=[vmem, vmem],
        compiler_params=params,
        cost_estimate=light,
        name="project",
    )(*arrays, out_weight)


def sides(n, n_tp, steps):
    me = lax.axis_index("ctx")
    my_tp = lax.axis_index("tp")
    share = n // n_tp
    found, near_count, away_count = [], jnp.int32(0), jnp.int32(0)
    for step in steps:
        owner = owner_of(me, step, n)
        away = lax.bitwise_xor(owner // share, my_tp) // 2 % 2
        found.append((owner, away, jnp.where(away == 1, away_count, near_count)))
        near_count = near_count + 1 - away
        away_count = away_count + away
    return found


def added(a, b):
    return a.astype(jnp.float32) + b.astype(jnp.float32)


def sort_kernel(n, n_tp, steps, *refs):
    *refs, stay_ref, send_ref, last_stay_ref, last_send_ref = refs
    count = len(refs) // 2
    places = [(a, b, i) for a, b in zip(refs[:count], refs[count:]) for i in range(a.shape[0])]
    full = stay_ref.shape[0]
    for (a, b, i), (_, away, rank) in zip(places, sides(n, n_tp, steps)):
        total = added(a[i], b[i]).astype(jnp.bfloat16)
        for side, out, last in ((0, stay_ref, last_stay_ref), (1, send_ref, last_send_ref)):

            @pl.when((away == side) & (rank < full))
            def _():
                out[rank] = total

            @pl.when((away == side) & (rank == full))
            def _():
                last[0] = total


def sort(n, n_tp, steps, sums):
    keeps, gots = zip(*sums)
    half, wide = keeps[0].shape[1:]
    many = jax.ShapeDtypeStruct((n // 2 - 1, half, wide), jnp.bfloat16)
    one = jax.ShapeDtypeStruct((1, half, wide), jnp.bfloat16)
    return pl.pallas_call(
        functools.partial(sort_kernel, n, n_tp, steps),
        out_shape=[many, many, one, one],
        in_specs=[vmem] * (2 * len(sums)),
        out_specs=[vmem] * 4,
        compiler_params=params,
        cost_estimate=light,
        name="sort",
    )(*keeps, *gots)


def last_kernel(n, n_tp, keep_ref, got_ref, stay_in, send_in, stay_ref, send_ref):
    ((_, away, _),) = sides(n, n_tp, (n // 2,))
    total = added(keep_ref[...], got_ref[...]).astype(jnp.bfloat16)
    stay_ref[...] = jnp.where(away == 0, total, stay_in[...])
    send_ref[...] = jnp.where(away == 1, total, send_in[...])


def place_last(n, n_tp, keep, got, stay, send):
    return pl.pallas_call(
        functools.partial(last_kernel, n, n_tp),
        out_shape=[jax.ShapeDtypeStruct(keep.shape, jnp.bfloat16)] * 2,
        in_specs=[vmem] * 4,
        out_specs=[vmem] * 2,
        compiler_params=params,
        cost_estimate=light,
        name="last",
    )(keep, got, stay, send)


def choose_kernel(n, n_tp, steps, *refs):
    stay, got, last_stay, last_got, mine_ref, give_ref = refs
    my_tp = lax.axis_index("tp")
    share = n // n_tp
    found = sides(n, n_tp, steps)
    full = stay.shape[0]
    for r in range(full + 1):
        owner = jnp.int32(0)
        for candidate, away, rank in found:
            owner = jnp.where((away == 0) & (rank == r), candidate, owner)
        if r < full:
            total = added(stay[r], got[r])
        else:
            total = added(last_stay[0], last_got[0])
        for out, block in ((mine_ref, my_tp), (give_ref, lax.bitwise_xor(my_tp, 1))):

            @pl.when(owner // share == block)
            def _():
                out[owner % share] = total.astype(out.dtype)


def choose(n, n_tp, steps, arrays):
    half, wide = arrays[0].shape[1:]
    return pl.pallas_call(
        functools.partial(choose_kernel, n, n_tp, steps),
        out_shape=[jax.ShapeDtypeStruct((n // n_tp, half, wide), jnp.bfloat16)] * 2,
        in_specs=[vmem] * 4,
        out_specs=[vmem, vmem],
        compiler_params=params,
        name="choose",
    )(*arrays)


def join_kernel(mine_ref, got_ref, out_ref):
    odd = lax.axis_index("tp") % 2
    count, half, _ = mine_ref.shape
    for low in range(2):
        first, second = (mine_ref, got_ref) if low == 0 else (got_ref, mine_ref)

        @pl.when(odd == low)
        def _():
            for i in range(count):
                out_ref[2 * i * half : (2 * i + 1) * half] = first[i]
                out_ref[(2 * i + 1) * half : (2 * i + 2) * half] = second[i]


def join(mine, got):
    count, half, wide = mine.shape
    return pl.pallas_call(
        join_kernel,
        out_shape=jax.ShapeDtypeStruct((2 * count * half, wide), jnp.bfloat16),
        in_specs=[vmem, vmem],
        out_specs=vmem,
        compiler_params=params,
        name="join",
    )(mine, got)


def after(array, token):
    return lax.optimization_barrier((array, token))[0]


def body(n, n_tp, queries, suffix_kv, cache_pool, hit_count, hit_slots, out_weight):
    tok = queries.shape[0]
    half = n // 2
    order = ring_order(n)
    right = [(order[i], order[(i + 1) % n]) for i in range(n)]
    left = [(b, a) for a, b in right]

    def send_both(pair, k, token):
        from_left, from_right = pair
        if token is not None:
            from_left = after(from_left, token)
            from_right = after(from_right, token)
        return lax.ppermute(from_left, "ctx", right), lax.ppermute(from_right, "ctx", left)

    def ring(own, visit, token):
        held = [send_both((a, a), k, None) for k, a in enumerate(own)]
        for step in range(1, half):
            token = visit(step - 1, arrived if step > 1 else None, token)
            arrived = held
            if step < half - 1:
                held = [send_both(arrived[k], k, token if step > 1 else None) for k in range(2)]
            else:
                held = (
                    lax.ppermute(after(arrived[0][0], token), "ctx", right),
                    lax.ppermute(after(arrived[1][1], token), "ctx", left),
                )
        token = visit(half - 1, arrived, token)
        return held, token

    def absorb(step, arrived, state):
        if step == 0:
            return flash(n, tok, queries, hit_count, ((0, 0), (1, 0)), own, (), False)
        turned, state = state[0], state[1:]
        for kind in range(2):
            pieces = ((kind, -step), (kind, step))
            state = flash(n, tok, turned, hit_count, pieces, arrived[kind], state, False)
        return [turned] + list(state)

    own = pick(hit_slots, cache_pool, suffix_kv)
    far, state = ring(own, absorb, None)
    attention = flash(
        n, tok, state[0], hit_count, ((0, half), (1, half)), far, tuple(state[1:]), True
    )

    swap = [(t, t ^ 1) for t in range(n_tp)]
    sums = []

    def reduce(arrays):
        keep, send = project(arrays, out_weight)
        sums.append((keep, lax.ppermute(send, "tp", swap)))
        return send

    def spread(step, arrived, token):
        if step == 0:
            return attention[0]
        (a_left, a_right), (b_left, b_right) = arrived
        arrays = (a_left, b_left, a_right, b_right)
        return reduce(tuple(attention) + arrays if step == 1 else arrays)

    def cross(stay, send):
        got = lax.ppermute(send, "tp", [(t, t ^ 2) for t in range(n_tp)])
        bit = 4
        while bit < n_tp:
            stay = added(stay, got).astype(jnp.bfloat16)
            got = lax.ppermute(stay, "tp", [(t, t ^ bit) for t in range(n_tp)])
            bit *= 2
        return stay, got

    far, _ = ring(attention, spread, None)
    steps = [0] + [s * d for d in range(1, half) for s in (-1, 1)] + [half]
    sums[0] = (after(sums[0][0], far), sums[0][1])
    stay, send, last_stay, last_send = sort(n, n_tp, steps[:-1], sums)
    stay, got = cross(stay, send)
    reduce(far)
    last_stay, last_send = place_last(n, n_tp, *sums[-1], last_stay, last_send)
    last_stay, last_got = cross(last_stay, last_send)
    mine, give = choose(n, n_tp, steps, (stay, got, last_stay, last_got))
    return join(mine, lax.ppermute(give, "tp", swap))


def solution(mesh):
    n, n_tp = mesh.shape["ctx"], mesh.shape["tp"]
    placed = (
        P("ctx", "tp"),
        P(None, "ctx", "tp"),
        P(None, "ctx", None, "tp"),
        P(),
        P("ctx", None),
        P("tp", "ctx"),
    )
    return jax.shard_map(
        functools.partial(body, n, n_tp),
        mesh=mesh,
        in_specs=placed,
        out_specs=P("tp", "ctx"),
        check_vma=False,
    )
```
